256 devices in a mesh: dp: 16 (over z_lo, y, core), vocab: 16 (over z_hi, x).
Axes of the slice: x: 4, y: 4, z: 8 (z_hi: 4, z_lo: 2; z = z_hi * 2 + z_lo), core: 2. Of those that a mesh axis runs over, the one named last changes fastest.
Arguments:
- hidden_rows: bfloat16 [2560, 8192], P('dp'), may hold values from -6 to 6
- translator: bfloat16 [8192, 8192], P(None, 'vocab'), may hold values from -0.0625 to 0.0625
- final_gain: float32 [8192], replicated, may hold values from 0.5 to 1.5
- unembed: bfloat16 [8192, 16384], P('dp', 'vocab'), may hold values from -8 to 8
- target_logits: bfloat16 [2560, 16384], P('dp', 'vocab'), may hold values from -40 to 300
Outputs:
- grad_translator: float32 [8192, 8192], P('dp', 'vocab')
- row_kl: float32 [2560], P('dp')
The draws below stay inside these ranges and needn't reach their ends.
All inputs are finite; a program needn't handle non-finite values.
Results may differ from the reference program's by a relative error of at most 0.0077.
Values may be sent and summed in bfloat16 or wider, within the bound.
No kernel may reach another device: no remote copies, remote signals or barrier semaphores. Data moves between devices by JAX's collectives and lax.ppermute only.
A program may use at most 128 MiB of HBM per device.

```python
import math
import jax
import jax.numpy as jnp
from jax import lax

D = 8192
V = 16384
ROWS = 2560


def draw_unembed(key, part):
    keys = jax.random.split(key, 2)
    col_scale = jnp.exp(jax.random.uniform(keys[1], (V,), minval=0.0, maxval=math.log(10.0)))
    base = jax.random.normal(keys[0], (D, V))
    weights = base * col_scale[None, :] * (0.06 / math.sqrt(D))
    return jnp.clip(weights, -8.0, 8.0).astype(jnp.bfloat16)


def draw_target_logits(key, part):
    keys = jax.random.split(key, 2)
    row_scale = jnp.exp(jax.random.uniform(keys[1], (ROWS, 1), minval=0.0, maxval=math.log(10.0)))
    values = jax.random.uniform(keys[0], (ROWS, V), minval=-3.464, maxval=3.464) * row_scale
    return jnp.clip(values, -40.0, 300.0).astype(jnp.bfloat16)


def spiked(drawn, stream_key, source, target, blocks, factor):
    owner, partner = [(jnp.arange(drawn.shape[position]) // (drawn.shape[position] // blocks)).reshape([-1 if axis == position else 1 for axis in range(drawn.ndim)]) for position in (source, target)]
    chosen = jax.random.permutation(stream_key, blocks)[partner]
    strong = (owner == chosen) | (owner == (partner + blocks // 2) % blocks)
    return jnp.where(strong, factor * drawn, drawn)


def levels(stream_key, extent, cuts, smallest, top_value):
    factor_of = 1.0
    for dim, parts in cuts:
        draws = jax.random.uniform(jax.random.fold_in(jax.random.fold_in(stream_key, 6), dim), (parts,), jnp.float32, smallest / len(cuts), top_value / len(cuts))
        factor_of = factor_of * jnp.repeat(jnp.exp(draws), extent[dim] // parts).reshape((-1,) + (1,) * (len(extent) - 1 - dim))
    return factor_of


def gaussian(rng, dims, spread, most, cuts=(), held_as=jnp.bfloat16):
    entries = spread * jax.random.normal(rng, dims, jnp.float32)
    if cuts:
        entries = entries * levels(rng, dims, cuts, -0.22, 0.18)
    return jnp.clip(entries, -most, most).astype(held_as)


def bell_draw_with(rng, shape, scale, reach, cuts, heavy, held_as=jnp.bfloat16):
    entries = scale * jax.random.normal(rng, shape, jnp.float32)
    if cuts:
        entries = entries * levels(rng, shape, cuts, -0.22, 0.18)
    return jnp.clip(spiked(entries, jax.random.fold_in(rng, 3), *heavy), -reach, reach).astype(held_as)


def setup_inputs(seed: int = 0) -> dict:
    splits = jax.random.split(jax.random.key(seed), 6)
    hidden_rows = bell_draw_with(splits[0], (ROWS, D), 1.0, 6.0, ((0, 16),), (0, 1, 16, 2.0))
    translator = gaussian(splits[1], (D, D), D ** -0.5, 0.0625, ((1, 16),))
    final_gain = jnp.clip(1.0 + 0.1 * jax.random.normal(splits[2], (D,), jnp.float32), 0.5, 1.5)
    unembed = draw_unembed(jax.random.fold_in(splits[5], 71), 0)
    target_logits = draw_target_logits(jax.random.fold_in(splits[5], 71), 0)
    return {"hidden_rows": hidden_rows, "translator": translator, "final_gain": final_gain, "unembed": unembed, "target_logits": target_logits}


EPSILON = 1e-05

def reference(hidden_rows, translator, final_gain, unembed, target_logits):
    translated = (hidden_rows.astype(jnp.float32) + jnp.dot(hidden_rows, translator, preferred_element_type=jnp.float32)).astype(jnp.bfloat16)
    trans_values = translated.astype(jnp.float32)
    inv_rms = lax.rsqrt(lax.optimization_barrier(jnp.mean(trans_values * trans_values, axis=1, keepdims=True)) + EPSILON)
    normed = (trans_values * inv_rms * final_gain).astype(jnp.bfloat16)
    logits = jnp.dot(normed, unembed, preferred_element_type=jnp.float32)
    target = target_logits.astype(jnp.float32)
    log_model = jax.nn.log_softmax(logits, axis=1)
    log_target = jax.nn.log_softmax(target, axis=1)
    prob_target = jnp.exp(log_target)
    row_kl = lax.optimization_barrier(jnp.sum(prob_target * (log_target - log_model), axis=1))
    grad_logits = (jnp.exp(log_model) - prob_target).astype(jnp.bfloat16)
    grad_normed = lax.dot_general(grad_logits, unembed, (((1,), (1,)), ((), ())), preferred_element_type=jnp.float32)
    scaled = grad_normed * final_gain
    inner = lax.optimization_barrier(jnp.mean(trans_values * scaled, axis=1, keepdims=True))
    grad_translated = (inv_rms * scaled - trans_values * inv_rms ** 3 * inner).astype(jnp.bfloat16)
    grad_translator = lax.dot_general(hidden_rows, grad_translated, (((0,), (0,)), ((), ())), preferred_element_type=jnp.float32)
    return (grad_translator, row_kl)
```

```python
import jax
import jax.numpy as jnp
from jax import lax
from jax.sharding import Mesh, PartitionSpec as P

EPSILON = 1e-05
SIZES = {"zl": 2, "y": 4, "c": 2, "zh": 4, "x": 4}
DP = ("zl", "y", "c")
VOCAB = ("zh", "x")
ROWS_A = 112


def shift(value, axis, step):
    size = SIZES[axis]
    return lax.ppermute(value, axis, [(i, (i + step) % size) for i in range(size)])


def own(blocks, axis, step):
    return lax.dynamic_index_in_dim(blocks, (lax.axis_index(axis) + step) % SIZES[axis], 0, False)


def gather_translated(part):
    rows, cols = part.shape
    zh, x = lax.axis_index("zh"), lax.axis_index("x")
    got = jnp.zeros((rows, 4 * cols), part.dtype)
    for k in range(4):
        piece = part if k == 0 else shift(part, "zh", k)
        got = lax.dynamic_update_slice(got, piece, (0, ((zh - k) % 4) * cols))
    whole = jnp.zeros((rows, 16 * cols), part.dtype)
    for k in range(4):
        piece = got if k == 0 else shift(got, "x", k)
        for z in range(4):
            whole = lax.dynamic_update_slice(
                whole, piece[:, z * cols : (z + 1) * cols], (0, (z * 4 + (x - k) % 4) * cols)
            )
    return whole


def reduce_pair(blocks, first, second):
    total = own(blocks, first, 0)
    for k in (1, 3, 2):
        total = total + shift(own(blocks, first, k), first, k)
    result = own(total, second, 0)
    for k in (1, 3, 2):
        result = result + shift(own(total, second, k), second, k)
    return result


def gather_rows(part):
    rows, cols = part.shape
    zl, y, c = lax.axis_index("zl"), lax.axis_index("y"), lax.axis_index("c")
    chip = jnp.zeros((8, rows, cols), part.dtype)
    for dz in range(2):
        for dy in (0, 1, 3, 2):
            piece = part
            if dz or dy:
                moves = [
                    (z * 4 + j, ((z + dz) % 2) * 4 + (j + dy) % 4) for z in range(2) for j in range(4)
                ]
                piece = lax.ppermute(part, ("zl", "y"), moves)
            chip = lax.dynamic_update_slice(
                chip, piece[None], (((zl - dz) % 2) * 4 + (y - dy) % 4, 0, 0)
            )
    other = shift(chip, "c", 1)
    mine_first = jnp.stack([chip, other], axis=1)
    other_first = jnp.stack([other, chip], axis=1)
    return jnp.where(c == 0, mine_first, other_first).reshape(16 * rows, cols)


def merge(s):
    def two(a, b):
        top, ttop = jnp.maximum(a[0], b[0]), jnp.maximum(a[3], b[3])
        out = [top, 0.0, 0.0, ttop, 0.0, 0.0, 0.0]
        for v in (a, b):
            dm, dt = v[0] - top, v[3] - ttop
            em, et = jnp.exp(dm), jnp.exp(dt)
            out[1] += em * v[1]
            out[2] += em * (v[2] + dm * v[1])
            out[4] += et * v[4]
            out[5] += et * (v[5] + dt * v[4])
            out[6] += et * (v[6] + dm * v[4])
        return jnp.stack(out + [jnp.zeros_like(top)])

    for axis in VOCAB:
        parts = [s] + [shift(s, axis, k) for k in (1, 3, 2)]
        s = two(two(parts[0], parts[3]), two(parts[1], parts[2]))
    return s


def local(hidden_rows, translator, final_gain, unembed, target_logits):
    row_count, feature_count = hidden_rows.shape
    col_count = translator.shape[1]
    first_col = lax.axis_index(VOCAB) * col_count
    full_unembed = lax.all_gather(unembed, DP, axis=0, tiled=True)
    own_inputs = lax.dynamic_slice_in_dim(hidden_rows, first_col, col_count, 1).astype(jnp.float32)
    own_part = (
        own_inputs + jnp.dot(hidden_rows, translator, preferred_element_type=jnp.float32)
    ).astype(jnp.bfloat16)
    translated = gather_translated(own_part)
    trans_values = translated.astype(jnp.float32)
    inv_rms = lax.rsqrt(jnp.mean(trans_values * trans_values, axis=1, keepdims=True) + EPSILON)
    normed = (trans_values * inv_rms * final_gain).astype(jnp.bfloat16)
    target = target_logits.astype(jnp.float32)
    target_top = jnp.max(target, axis=1)
    target_off = target - target_top[:, None]
    target_exp = jnp.exp(target_off)
    target_total = jnp.sum(target_exp, axis=1)
    target_mean = jnp.sum(target_exp * target_off, axis=1)
    logits = jnp.dot(normed, full_unembed, preferred_element_type=jnp.float32)
    model_top = jnp.max(logits, axis=1)
    model_off = logits - model_top[:, None]
    model_exp = jnp.exp(model_off)
    mine = jnp.stack(
        [
            model_top,
            jnp.sum(model_exp, axis=1),
            jnp.sum(model_exp * model_off, axis=1),
            target_top,
            target_total,
            target_mean,
            jnp.sum(target_exp * model_off, axis=1),
            jnp.zeros_like(model_top),
        ]
    )
    whole = merge(mine)
    model_sum, target_sum = whole[1], whole[4]
    row_kl = (
        (whole[5] - whole[6]) / target_sum - jnp.log(target_sum) + jnp.log(model_sum)
    )
    inner = (whole[2] / model_sum - whole[6] / target_sum) / (inv_rms[:, 0] * feature_count)
    prob_model = jnp.exp(logits - whole[0][:, None]) / model_sum[:, None]
    prob_target = jnp.exp(target - whole[3][:, None]) / target_sum[:, None]
    grad_logits = (prob_model - prob_target).astype(jnp.bfloat16)
    hidden_late, grad_logits = lax.optimization_barrier((hidden_rows, grad_logits))
    input_slices = lax.all_to_all(hidden_late, DP, split_axis=1, concat_axis=0, tiled=True)
    grad_partial = lax.dot_general(
        grad_logits, full_unembed, (((1,), (1,)), ((), ())), preferred_element_type=jnp.float32
    )
    blocks = grad_partial.reshape(row_count, 4, 4, col_count)
    part_a = reduce_pair(blocks[:ROWS_A].transpose(2, 1, 0, 3), "x", "zh")
    part_b = reduce_pair(blocks[ROWS_A:].transpose(1, 2, 0, 3), "zh", "x")
    grad_cols = jnp.concatenate([part_a, part_b], axis=0)
    gain_cols = lax.dynamic_slice_in_dim(final_gain, first_col, col_count, 0)
    value_cols = own_part.astype(jnp.float32)
    scaled = grad_cols * gain_cols
    grad_translated = (inv_rms * scaled - value_cols * inv_rms**3 * inner[:, None]).astype(
        jnp.bfloat16
    )
    grad_translator = lax.dot_general(
        input_slices,
        gather_rows(grad_translated),
        (((0,), (0,)), ((), ())),
        preferred_element_type=jnp.float32,
    )
    return (grad_translator, row_kl)


def solution(mesh):
    split = Mesh(mesh.devices.reshape(tuple(SIZES.values())), tuple(SIZES))
    return jax.shard_map(
        local,
        mesh=split,
        in_specs=(P(DP, None), P(None, VOCAB), P(), P(DP, VOCAB), P(DP, VOCAB)),
        out_specs=(P(DP, VOCAB), P(DP)),
        check_vma=False,
    )
```

```python
import functools

import jax
import jax.numpy as jnp
from jax import lax
from jax.experimental import pallas as pl
from jax.experimental.pallas import tpu as pltpu
from jax.sharding import Mesh, PartitionSpec as P

EPSILON = 1e-05
SIZES = {"zl": 2, "y": 4, "c": 2, "zh": 4, "x": 4}
DP = ("zl", "y", "c")
VOCAB = ("zh", "x")
ROWS_A = 112


def shift(value, axis, step):
    size = SIZES[axis]
    return lax.ppermute(value, axis, [(i, (i + step) % size) for i in range(size)])


def gather_translated(part):
    rows, cols = part.shape
    zh, x = lax.axis_index("zh"), lax.axis_index("x")
    got = jnp.zeros((rows, 4 * cols), part.dtype)
    for k in range(4):
        piece = part if k == 0 else shift(part, "zh", k)
        got = lax.dynamic_update_slice(got, piece, (0, ((zh - k) % 4) * cols))
    whole = jnp.zeros((rows, 16 * cols), part.dtype)
    for k in range(4):
        piece = got if k == 0 else shift(got, "x", k)
        for z in range(4):
            whole = lax.dynamic_update_slice(
                whole, piece[:, z * cols : (z + 1) * cols], (0, (z * 4 + (x - k) % 4) * cols)
            )
    return whole


def reduce_pair(blocks, first, second):
    total = blocks[0]
    for k in (1, 3, 2):
        total = total + shift(blocks[k], first, k)
    result = total[0]
    for k in (1, 3, 2):
        result = result + shift(total[k], second, k)
    return result


def gather_unembed(part):
    half = part.shape[0] // 2
    partner = shift(part, "zl", 1)
    pieces = []
    for dz, own_part in enumerate((part, partner)):
        low, high = shift(own_part, "y", 1), shift(own_part, "y", 3)
        far_top, far_end = shift(low[:half], "y", 1), shift(high[half:], "y", 3)
        pieces += [
            (own_part, dz, 0, 0),
            (low, dz, 1, 0),
            (high, dz, 3, 0),
            (far_top, dz, 2, 0),
            (far_end, dz, 2, half),
        ]
    out = []
    for value, dz, dy, row in pieces:
        out += [(value, dz, dy, 0, row), (shift(value, "c", 1), dz, dy, 1, row)]
    return out


def position():
    return jnp.stack([lax.axis_index(a) for a in SIZES]).astype(jnp.int32)


def piece_block(place, spot):
    dz, dy, dc, _ = spot
    zl = (place[0] + (2 - dz)) % 2
    y = (place[1] + (4 - dy)) % 4
    c = (place[2] + (2 - dc)) % 2
    return zl * 8 + y * 2 + c


def forward_kernel(heights, spots, block, place, normed, *refs):
    count = len(heights)
    pieces, out, held, sems = refs[:count], refs[count], refs[count + 1], refs[count + 2]
    copies, start = [], 0
    for p, height in enumerate(heights):
        copies.append(
            pltpu.make_async_copy(pieces[p], held.at[pl.ds(start, height)], sems.at[p])
        )
        copies[-1].start()
        start += height
    start = 0
    for p, height in enumerate(heights):
        copies[p].wait()
        first = piece_block(place, spots[p]) * block + spots[p][3]
        cols = normed[:, pl.ds(pl.multiple_of(first, 256), height)]
        term = jnp.dot(cols, held[pl.ds(start, height), :], preferred_element_type=jnp.float32)
        if p:
            out[...] += term
        else:
            out[...] = term
        start += height


def forward(normed, pieces, block):
    heights = [p[0].shape[0] for p in pieces]
    rows, cols = normed.shape[0], pieces[0][0].shape[1]
    spots = [p[1:] for p in pieces]
    return pl.pallas_call(
        functools.partial(forward_kernel, heights, spots, block),
        out_shape=jax.ShapeDtypeStruct((rows, cols), jnp.float32),
        in_specs=[
            pl.BlockSpec(memory_space=pltpu.SMEM),
            pl.BlockSpec(memory_space=pltpu.VMEM),
        ]
        + [pl.BlockSpec(memory_space=pl.ANY)] * len(pieces),
        out_specs=pl.BlockSpec(memory_space=pltpu.VMEM),
        scratch_shapes=[
            pltpu.VMEM((sum(heights), cols), jnp.bfloat16),
            pltpu.SemaphoreType.DMA((len(pieces),)),
        ],
        compiler_params=pltpu.CompilerParams(vmem_limit_bytes=36 * 2**20),
        cost_estimate=pl.CostEstimate(
            flops=2 * rows * cols * sum(heights), bytes_accessed=2 * cols * sum(heights), transcendentals=0
        ),
        name="forward",
    )(position(), normed, *[p[0] for p in pieces])


def backward_kernel(heights, spots, place, grad, *refs):
    count = len(heights)
    pieces, outs_a, outs_b = refs[:count], refs[count : count + 4], refs[count + 4 : count + 8]
    held, made, in_sems, a_sems, b_sems = refs[count + 8 :]
    copies, start = [], 0
    for p, height in enumerate(heights):
        copies.append(
            pltpu.make_async_copy(pieces[p], held.at[pl.ds(start, height)], in_sems.at[p])
        )
        copies[-1].start()
        start += height
    start = 0

    def send_a(p, k, at):
        return pltpu.make_async_copy(
            made.at[p, pl.ds(0, ROWS_A), pl.ds(0, heights[p])],
            outs_a[k].at[at, :, pl.ds(spots[p][3], heights[p])],
            a_sems.at[p],
        )

    def send_b(p, k, at):
        return pltpu.make_async_copy(
            made.at[p, pl.ds(ROWS_A, made.shape[1] - ROWS_A), pl.ds(0, heights[p])],
            outs_b[k].at[at, :, pl.ds(spots[p][3], heights[p])],
            b_sems.at[p],
        )

    for p, height in enumerate(heights):
        copies[p].wait()
        made[p, :, pl.ds(0, height)] = lax.dot_general(
            grad[...],
            held[pl.ds(start, height), :],
            (((1,), (1,)), ((), ())),
            preferred_element_type=jnp.float32,
        )
        start += height
        owner = piece_block(place, spots[p])
        kx_at = (owner % 4 + 4 - place[4]) % 4
        kz_at = (owner // 4 + 4 - place[3]) % 4
        for k in range(4):

            @pl.when(kx_at == k)
            def _():
                send_a(p, k, kz_at).start()

            @pl.when(kz_at == k)
            def _():
                send_b(p, k, kx_at).start()

    for p in range(count):
        send_a(p, 0, 0).wait()
        send_b(p, 0, 0).wait()


def backward(grad, pieces, block):
    heights = [p[0].shape[0] for p in pieces]
    spots = [p[1:] for p in pieces]
    rows, cols = grad.shape
    out = pl.pallas_call(
        functools.partial(backward_kernel, heights, spots),
        out_shape=[jax.ShapeDtypeStruct((4, ROWS_A, block), jnp.float32)] * 4
        + [jax.ShapeDtypeStruct((4, rows - ROWS_A, block), jnp.float32)] * 4,
        in_specs=[
            pl.BlockSpec(memory_space=pltpu.SMEM),
            pl.BlockSpec(memory_space=pltpu.VMEM),
        ]
        + [pl.BlockSpec(memory_space=pl.ANY)] * len(pieces),
        out_specs=[pl.BlockSpec(memory_space=pl.ANY)] * 8,
        scratch_shapes=[
            pltpu.VMEM((sum(heights), cols), jnp.bfloat16),
            pltpu.VMEM((len(pieces), rows, block), jnp.float32),
            pltpu.SemaphoreType.DMA((len(pieces),)),
            pltpu.SemaphoreType.DMA((len(pieces),)),
            pltpu.SemaphoreType.DMA((len(pieces),)),
        ],
        compiler_params=pltpu.CompilerParams(vmem_limit_bytes=36 * 2**20),
        cost_estimate=pl.CostEstimate(
            flops=2 * rows * cols * sum(heights),
            bytes_accessed=2 * cols * sum(heights) + 4 * rows * sum(heights),
            transcendentals=0,
        ),
        name="backward",
    )(position(), grad, *[p[0] for p in pieces])
    return out[:4], out[4:]


def gather_rows(part):
    rows, cols = part.shape
    zl, y, c = lax.axis_index("zl"), lax.axis_index("y"), lax.axis_index("c")
    chip = jnp.zeros((8, rows, cols), part.dtype)
    for dz in range(2):
        for dy in (0, 1, 3, 2):
            piece = part
            if dz or dy:
                moves = [
                    (z * 4 + j, ((z + dz) % 2) * 4 + (j + dy) % 4) for z in range(2) for j in range(4)
                ]
                piece = lax.ppermute(part, ("zl", "y"), moves)
            chip = lax.dynamic_update_slice(
                chip, piece[None], (((zl - dz) % 2) * 4 + (y - dy) % 4, 0, 0)
            )
    other = shift(chip, "c", 1)
    mine_first = jnp.stack([chip, other], axis=1)
    other_first = jnp.stack([other, chip], axis=1)
    return jnp.where(c == 0, mine_first, other_first).reshape(16 * rows, cols)


def merge(s):
    def two(a, b):
        top, ttop = jnp.maximum(a[0], b[0]), jnp.maximum(a[3], b[3])
        out = [top, 0.0, 0.0, ttop, 0.0, 0.0, 0.0]
        for v in (a, b):
            dm, dt = v[0] - top, v[3] - ttop
            em, et = jnp.exp(dm), jnp.exp(dt)
            out[1] += em * v[1]
            out[2] += em * (v[2] + dm * v[1])
            out[4] += et * v[4]
            out[5] += et * (v[5] + dt * v[4])
            out[6] += et * (v[6] + dm * v[4])
        return jnp.stack(out + [jnp.zeros_like(top)])

    for axis in VOCAB:
        parts = [s] + [shift(s, axis, k) for k in (1, 3, 2)]
        s = two(two(parts[0], parts[3]), two(parts[1], parts[2]))
    return s


def local(hidden_rows, translator, final_gain, unembed, target_logits):
    row_count, feature_count = hidden_rows.shape
    col_count = translator.shape[1]
    first_col = lax.axis_index(VOCAB) * col_count
    pieces = gather_unembed(unembed)
    own_inputs = lax.dynamic_slice_in_dim(hidden_rows, first_col, col_count, 1).astype(jnp.float32)
    own_part = (
        own_inputs + jnp.dot(hidden_rows, translator, preferred_element_type=jnp.float32)
    ).astype(jnp.bfloat16)
    translated = gather_translated(own_part)
    trans_values = translated.astype(jnp.float32)
    inv_rms = lax.rsqrt(jnp.mean(trans_values * trans_values, axis=1, keepdims=True) + EPSILON)
    normed = (trans_values * inv_rms * final_gain).astype(jnp.bfloat16)
    target = target_logits.astype(jnp.float32)
    target_top = jnp.max(target, axis=1)
    target_off = target - target_top[:, None]
    target_exp = jnp.exp(target_off)
    target_total = jnp.sum(target_exp, axis=1)
    target_mean = jnp.sum(target_exp * target_off, axis=1)
    logits = forward(normed, pieces, unembed.shape[0])
    model_top = jnp.max(logits, axis=1)
    model_off = logits - model_top[:, None]
    model_exp = jnp.exp(model_off)
    mine = jnp.stack(
        [
            model_top,
            jnp.sum(model_exp, axis=1),
            jnp.sum(model_exp * model_off, axis=1),
            target_top,
            target_total,
            target_mean,
            jnp.sum(target_exp * model_off, axis=1),
            jnp.zeros_like(model_top),
        ]
    )
    whole = merge(mine)
    model_sum, target_sum = whole[1], whole[4]
    row_kl = (
        (whole[5] - whole[6]) / target_sum - jnp.log(target_sum) + jnp.log(model_sum)
    )
    inner = (whole[2] / model_sum - whole[6] / target_sum) / (inv_rms[:, 0] * feature_count)
    prob_model = jnp.exp(logits - whole[0][:, None]) / model_sum[:, None]
    prob_target = jnp.exp(target - whole[3][:, None]) / target_sum[:, None]
    grad_logits = (prob_model - prob_target).astype(jnp.bfloat16)
    hidden_late, grad_logits = lax.optimization_barrier((hidden_rows, grad_logits))
    input_slices = lax.all_to_all(hidden_late, DP, split_axis=1, concat_axis=0, tiled=True)
    to_a, to_b = backward(grad_logits, pieces, unembed.shape[0])
    part_a = reduce_pair(to_a, "x", "zh")
    part_b = reduce_pair(to_b, "zh", "x")
    grad_cols = jnp.concatenate([part_a, part_b], axis=0)
    gain_cols = lax.dynamic_slice_in_dim(final_gain, first_col, col_count, 0)
    value_cols = own_part.astype(jnp.float32)
    scaled = grad_cols * gain_cols
    grad_translated = (inv_rms * scaled - value_cols * inv_rms**3 * inner[:, None]).astype(
        jnp.bfloat16
    )
    grad_translator = lax.dot_general(
        input_slices,
        gather_rows(grad_translated),
        (((0,), (0,)), ((), ())),
        preferred_element_type=jnp.float32,
    )
    return (grad_translator, row_kl)


def solution(mesh):
    split = Mesh(mesh.devices.reshape(tuple(SIZES.values())), tuple(SIZES))
    return jax.shard_map(
        local,
        mesh=split,
        in_specs=(P(DP, None), P(None, VOCAB), P(), P(DP, VOCAB), P(DP, VOCAB)),
        out_specs=(P(DP, VOCAB), P(DP)),
        check_vma=False,
    )
```

```python
import functools

import jax
import jax.numpy as jnp
from jax import lax
from jax.experimental import pallas as pl
from jax.experimental.pallas import tpu as pltpu
from jax.sharding import Mesh, PartitionSpec as P

EPSILON = 1e-05
SIZES = {"zl": 2, "y": 4, "c": 2, "zh": 4, "x": 4}
DP = ("zl", "y", "c")
VOCAB = ("zh", "x")


def shift(value, axis, step):
    size = SIZES[axis]
    return lax.ppermute(value, axis, [(i, (i + step) % size) for i in range(size)])


def gather_translated(part):
    rows, cols = part.shape
    zh, x = lax.axis_index("zh"), lax.axis_index("x")
    got = jnp.zeros((rows, 4 * cols), part.dtype)
    for k in range(4):
        piece = part if k == 0 else shift(part, "zh", k)
        got = lax.dynamic_update_slice(got, piece, (0, ((zh - k) % 4) * cols))
    whole = jnp.zeros((rows, 16 * cols), part.dtype)
    for k in range(4):
        piece = got if k == 0 else shift(got, "x", k)
        for z in range(4):
            whole = lax.dynamic_update_slice(
                whole, piece[:, z * cols : (z + 1) * cols], (0, (z * 4 + (x - k) % 4) * cols)
            )
    return whole


def backward_kernel(kz, place, grad, unembed, *refs):
    outs, held, sems = refs[:4], refs[4], refs[5]
    block = held.shape[1]
    order = (2, 1, 3, 0)
    copies = []
    for kx in order:
        owner = ((place[0] + kz) % 4) * 4 + (place[1] + kx) % 4
        first = pl.multiple_of(owner * block, block)
        copies.append(
            pltpu.make_async_copy(unembed.at[pl.ds(first, block)], held.at[kx], sems.at[kx])
        )
        copies[-1].start()
    for kx, copy in zip(order, copies):
        copy.wait()
        outs[kx][...] = lax.dot_general(
            grad[...], held[kx], (((1,), (1,)), ((), ())), preferred_element_type=jnp.float32
        )


def backward(kz, grad, unembed, block):
    rows, cols = grad.shape
    place = jnp.stack([lax.axis_index("zh"), lax.axis_index("x")]).astype(jnp.int32)
    return pl.pallas_call(
        functools.partial(backward_kernel, kz),
        out_shape=[jax.ShapeDtypeStruct((rows, block), jnp.float32)] * 4,
        in_specs=[
            pl.BlockSpec(memory_space=pltpu.SMEM),
            pl.BlockSpec(memory_space=pltpu.VMEM),
            pl.BlockSpec(memory_space=pltpu.HBM),
        ],
        out_specs=[pl.BlockSpec(memory_space=pltpu.VMEM)] * 4,
        scratch_shapes=[
            pltpu.VMEM((4, block, cols), jnp.bfloat16),
            pltpu.SemaphoreType.DMA((4,)),
        ],
        compiler_params=pltpu.CompilerParams(vmem_limit_bytes=50 * 2**20),
        cost_estimate=pl.CostEstimate(
            flops=8 * rows * cols * block,
            bytes_accessed=8 * cols * block + 16 * rows * block,
            transcendentals=0,
        ),
        name="backward",
    )(place, grad, unembed)


def merge_kernel(a, b, c, d, out):
    groups = (a, b, c, d)
    top = jnp.maximum(jnp.maximum(a[0:1], b[0:1]), jnp.maximum(c[0:1], d[0:1]))
    ttop = jnp.maximum(jnp.maximum(a[3:4], b[3:4]), jnp.maximum(c[3:4], d[3:4]))
    sums = [jnp.zeros_like(top) for _ in range(5)]
    for v in groups:
        dm, dt = v[0:1] - top, v[3:4] - ttop
        em, et = jnp.exp(dm), jnp.exp(dt)
        sums[0] += em * v[1:2]
        sums[1] += em * (v[2:3] + dm * v[1:2])
        sums[2] += et * v[4:5]
        sums[3] += et * (v[5:6] + dt * v[4:5])
        sums[4] += et * (v[6:7] + dm * v[4:5])
    for row, value in enumerate((top, sums[0], sums[1], ttop, sums[2], sums[3], sums[4], top)):
        out[row : row + 1] = value


def merge(s):
    for axis in VOCAB:
        far, low, high = shift(s, axis, 2), shift(s, axis, 1), shift(s, axis, 3)
        s = pl.pallas_call(
            merge_kernel,
            out_shape=jax.ShapeDtypeStruct(s.shape, s.dtype),
            in_specs=[pl.BlockSpec(memory_space=pltpu.VMEM)] * 4,
            out_specs=pl.BlockSpec(memory_space=pltpu.VMEM),
            compiler_params=pltpu.CompilerParams(vmem_limit_bytes=2**20),
            name="merge",
        )(s, low, high, far)
    return s


def gather_rows(part):
    rows, cols = part.shape
    y = lax.axis_index("y")
    chip = jnp.zeros((4, 2, rows, cols), part.dtype)
    for dz, dy in ((1, 2), (0, 2), (1, 1), (1, 3), (0, 1), (0, 3), (1, 0), (0, 0)):
        piece = part
        if dz or dy:
            moves = [
                (z * 4 + j, ((z + dz) % 2) * 4 + (j + dy) % 4) for z in range(2) for j in range(4)
            ]
            piece = lax.ppermute(part, ("zl", "y"), moves)
        chip = lax.dynamic_update_slice(chip, piece[None, None], ((y - dy) % 4, dz, 0, 0))
    chip = chip.reshape(8 * rows, cols)
    return chip, shift(chip, "c", 1)


def local(hidden_rows, translator, final_gain, unembed, target_logits):
    row_count, feature_count = hidden_rows.shape
    col_count = translator.shape[1]
    first_col = lax.axis_index(VOCAB) * col_count
    zl, c = lax.axis_index("zl"), lax.axis_index("c")
    half = feature_count // 2
    hidden_near = lax.dynamic_slice_in_dim(hidden_rows, zl * half, half, 1)
    hidden_far = shift(lax.dynamic_slice_in_dim(hidden_rows, (1 - zl) * half, half, 1), "zl", 1)
    hidden_both = jnp.concatenate([hidden_near, hidden_far], axis=0)
    full_unembed = lax.all_gather(unembed, DP, axis=0, tiled=True)
    own_inputs = lax.dynamic_slice_in_dim(hidden_rows, first_col, col_count, 1).astype(jnp.float32)
    own_part = (
        own_inputs + jnp.dot(hidden_rows, translator, preferred_element_type=jnp.float32)
    ).astype(jnp.bfloat16)
    translated = gather_translated(own_part)
    trans_values = translated.astype(jnp.float32)
    inv_rms = lax.rsqrt(jnp.mean(trans_values * trans_values, axis=1, keepdims=True) + EPSILON)
    normed = (trans_values * inv_rms * final_gain).astype(jnp.bfloat16)
    normed, hidden_both = lax.optimization_barrier((normed, hidden_both))
    target = target_logits.astype(jnp.float32)
    target_top = jnp.max(target, axis=1)
    target_off = target - target_top[:, None]
    target_exp = jnp.exp(target_off)
    target_total = jnp.sum(target_exp, axis=1)
    target_mean = jnp.sum(target_exp * target_off, axis=1)
    logits = jnp.dot(normed, full_unembed, preferred_element_type=jnp.float32)
    model_top = jnp.max(logits, axis=1)
    model_off = logits - model_top[:, None]
    model_exp = jnp.exp(model_off)
    mine = jnp.stack(
        [
            model_top,
            jnp.sum(model_exp, axis=1),
            jnp.sum(model_exp * model_off, axis=1),
            target_top,
            target_total,
            target_mean,
            jnp.sum(target_exp * model_off, axis=1),
            jnp.zeros_like(model_top),
        ]
    )
    whole = merge(mine)
    model_sum, target_sum = whole[1], whole[4]
    row_kl = (
        (whole[5] - whole[6]) / target_sum - jnp.log(target_sum) + jnp.log(model_sum)
    )
    inner = (whole[2] / model_sum - whole[6] / target_sum) / (inv_rms[:, 0] * feature_count)
    prob_model = jnp.exp(logits - whole[0][:, None]) / model_sum[:, None]
    prob_target = jnp.exp(target - whole[3][:, None]) / target_sum[:, None]
    grad_logits = (prob_model - prob_target).astype(jnp.bfloat16)
    sums, moved = [], []
    for step, kz in enumerate((2, 1, 3, 0)):
        if step >= 2:
            grad_logits, sums[step - 2] = lax.optimization_barrier((grad_logits, sums[step - 2]))
            moved.append(shift(sums[step - 2], "zh", (2, 1)[step - 2]))
        blocks = list(backward(kz, grad_logits, full_unembed, col_count))
        if not step:
            blocks[3], hidden_both = lax.optimization_barrier((blocks[3], hidden_both))
            slices = lax.all_to_all(hidden_both, ("y", "c"), split_axis=1, concat_axis=0, tiled=True)
        total = blocks[0]
        for kx in (2, 1, 3):
            total = total + shift(blocks[kx], "x", kx)
        sums.append(total)
    sums[2], moved[0] = lax.optimization_barrier((sums[2], moved[0]))
    moved.append(shift(sums[2], "zh", 3))
    sums[3], moved[1], slices = lax.optimization_barrier((sums[3], moved[1], slices))
    grad_cols = sums[3] + moved[0] + moved[1] + moved[2]
    slices = slices.reshape(4, 2, 2 * row_count, col_count)
    slices_own = lax.dynamic_index_in_dim(slices, c, 1, False).reshape(8 * row_count, col_count)
    slices_other = lax.dynamic_index_in_dim(slices, 1 - c, 1, False).reshape(8 * row_count, col_count)
    gain_cols = lax.dynamic_slice_in_dim(final_gain, first_col, col_count, 0)
    value_cols = own_part.astype(jnp.float32)
    scaled = grad_cols * gain_cols
    grad_translated = (inv_rms * scaled - value_cols * inv_rms**3 * inner[:, None]).astype(
        jnp.bfloat16
    )
    chip, other = gather_rows(grad_translated)
    over_rows = (((0,), (0,)), ((), ()))
    grad_translator = lax.dot_general(
        slices_own, chip, over_rows, preferred_element_type=jnp.float32
    )
    grad_translator, other = lax.optimization_barrier((grad_translator, other))
    grad_translator += lax.dot_general(
        slices_other, other, over_rows, preferred_element_type=jnp.float32
    )
    return (grad_translator, row_kl)


def solution(mesh):
    split = Mesh(mesh.devices.reshape(tuple(SIZES.values())), tuple(SIZES))
    return jax.shard_map(
        local,
        mesh=split,
        in_specs=(P(DP, None), P(None, VOCAB), P(), P(DP, VOCAB), P(DP, VOCAB)),
        out_specs=(P(DP, VOCAB), P(DP)),
        check_vma=False,
    )
```

```python
import functools

import jax
import jax.numpy as jnp
from jax import lax
from jax.experimental import pallas as pl
from jax.experimental.pallas import tpu as pltpu
from jax.sharding import Mesh, PartitionSpec as P

EPSILON = 1e-05
SIZES = {"zl": 2, "y": 4, "c": 2, "zh": 4, "x": 4}
DP = ("zl", "y", "c")
VOCAB = ("zh", "x")


def shift(value, axis, step):
    size = SIZES[axis]
    return lax.ppermute(value, axis, [(i, (i + step) % size) for i in range(size)])


def gather_translated(part):
    rows, cols = part.shape
    zh, x = lax.axis_index("zh"), lax.axis_index("x")
    got = jnp.zeros((rows, 4 * cols), part.dtype)
    for k in range(4):
        piece = part if k == 0 else shift(part, "zh", k)
        got = lax.dynamic_update_slice(got, piece, (0, ((zh - k) % 4) * cols))
    whole = jnp.zeros((rows, 16 * cols), part.dtype)
    for k in range(4):
        piece = got if k == 0 else shift(got, "x", k)
        for z in range(4):
            whole = lax.dynamic_update_slice(
                whole, piece[:, z * cols : (z + 1) * cols], (0, (z * 4 + (x - k) % 4) * cols)
            )
    return whole


def gather_unembed(part):
    half = part.shape[0] // 2
    first = lax.all_gather(part[:half], DP, axis=0, tiled=True)
    mine = part[half:]
    pair = jnp.concatenate([mine, shift(mine, "zl", 1)], axis=0)
    second = []
    for dy in range(4):
        piece = shift(pair, "y", dy) if dy else pair
        second += [piece, shift(piece, "c", 1)]
    return first, second


def position():
    return jnp.stack([lax.axis_index(a) for a in SIZES]).astype(jnp.int32)


def forward_kernel(place, normed, first, *refs):
    second, out, held, sems, late_sems = refs[:8], refs[8], refs[9], refs[10], refs[11]
    half = held.shape[0] // 32
    late, copies = [], []
    for p in range(8):
        for dz in range(2):
            owner = (
                ((place[0] + dz) % 2) * 8 + ((place[1] + 4 - p // 2) % 4) * 2 + (place[2] + p % 2) % 2
            )
            at = pl.multiple_of(owner * (2 * half) + half, half)
            late.append(
                pltpu.make_async_copy(
                    second[p].at[pl.ds(dz * half, half)],
                    held.at[pl.ds(at, half)],
                    late_sems.at[2 * p + dz],
                )
            )
            late[-1].start()
    for i in range(16):
        copies.append(
            pltpu.make_async_copy(
                first.at[pl.ds(i * half, half)], held.at[pl.ds(2 * i * half, half)], sems.at[i]
            )
        )
        copies[-1].start()
    for copy in late:
        copy.wait()
    for i, copy in enumerate(copies):
        copy.wait()
        rows = pl.ds(2 * i * half, 2 * half)
        term = jnp.dot(normed[:, rows], held[rows, :], preferred_element_type=jnp.float32)
        if i:
            out[...] += term
        else:
            out[...] = term


def forward(normed, first, second):
    rows, features = normed.shape
    cols = first.shape[1]
    return pl.pallas_call(
        forward_kernel,
        out_shape=jax.ShapeDtypeStruct((rows, cols), jnp.float32),
        in_specs=[
            pl.BlockSpec(memory_space=pltpu.SMEM),
            pl.BlockSpec(memory_space=pltpu.VMEM),
        ]
        + [pl.BlockSpec(memory_space=pltpu.HBM)] * 9,
        out_specs=pl.BlockSpec(memory_space=pltpu.VMEM),
        scratch_shapes=[
            pltpu.VMEM((features, cols), jnp.bfloat16),
            pltpu.SemaphoreType.DMA((16,)),
            pltpu.SemaphoreType.DMA((16,)),
        ],
        compiler_params=pltpu.CompilerParams(vmem_limit_bytes=54 * 2**20),
        cost_estimate=pl.CostEstimate(
            flops=2 * rows * cols * features, bytes_accessed=2 * cols * features, transcendentals=0
        ),
        name="forward",
    )(position(), normed, first, *second)


def backward_kernel(kz, place, grad, first, *refs):
    second, outs, held, sems, late_sems = refs[:8], refs[8:12], refs[12], refs[13], refs[14]
    block = held.shape[1]
    half = block // 2
    order = (2, 1, 3, 0)

    def early(owner, kx):
        return pltpu.make_async_copy(
            first.at[pl.ds(pl.multiple_of(owner * half, half), half)],
            held.at[kx, pl.ds(0, half)],
            sems.at[kx],
        )

    def late(p, dz, kx):
        return pltpu.make_async_copy(
            second[p].at[pl.ds(pl.multiple_of(dz * half, half), half)],
            held.at[kx, pl.ds(half, half)],
            late_sems.at[kx],
        )

    for kx in order:
        owner = ((place[3] + kz) % 4) * 4 + (place[4] + kx) % 4
        early(owner, kx).start()
        dz = (owner // 8 + place[0]) % 2
        dy = (place[1] + 4 - (owner // 2) % 4) % 4
        which = dy * 2 + (owner + place[2]) % 2
        for p in range(8):

            @pl.when(which == p)
            def _():
                late(p, dz, kx).start()

    for kx in order:
        early(0, kx).wait()
        late(0, 0, kx).wait()
        outs[kx][...] = lax.dot_general(
            grad[...], held[kx], (((1,), (1,)), ((), ())), preferred_element_type=jnp.float32
        )


def backward(kz, grad, first, second, block):
    rows, cols = grad.shape
    return pl.pallas_call(
        functools.partial(backward_kernel, kz),
        out_shape=[jax.ShapeDtypeStruct((rows, block), jnp.float32)] * 4,
        in_specs=[
            pl.BlockSpec(memory_space=pltpu.SMEM),
            pl.BlockSpec(memory_space=pltpu.VMEM),
        ]
        + [pl.BlockSpec(memory_space=pltpu.HBM)] * 9,
        out_specs=[pl.BlockSpec(memory_space=pltpu.VMEM)] * 4,
        scratch_shapes=[
            pltpu.VMEM((4, block, cols), jnp.bfloat16),
            pltpu.SemaphoreType.DMA((4,)),
            pltpu.SemaphoreType.DMA((4,)),
        ],
        compiler_params=pltpu.CompilerParams(vmem_limit_bytes=50 * 2**20),
        cost_estimate=pl.CostEstimate(
            flops=8 * rows * cols * block,
            bytes_accessed=8 * cols * block + 16 * rows * block,
            transcendentals=0,
        ),
        name="backward",
    )(position(), grad, first, *second)


def merge_kernel(a, b, c, d, out):
    groups = (a, b, c, d)
    top = jnp.maximum(jnp.maximum(a[0:1], b[0:1]), jnp.maximum(c[0:1], d[0:1]))
    ttop = jnp.maximum(jnp.maximum(a[3:4], b[3:4]), jnp.maximum(c[3:4], d[3:4]))
    sums = [jnp.zeros_like(top) for _ in range(5)]
    for v in groups:
        dm, dt = v[0:1] - top, v[3:4] - ttop
        em, et = jnp.exp(dm), jnp.exp(dt)
        sums[0] += em * v[1:2]
        sums[1] += em * (v[2:3] + dm * v[1:2])
        sums[2] += et * v[4:5]
        sums[3] += et * (v[5:6] + dt * v[4:5])
        sums[4] += et * (v[6:7] + dm * v[4:5])
    for row, value in enumerate((top, sums[0], sums[1], ttop, sums[2], sums[3], sums[4], top)):
        out[row : row + 1] = value


def merge(s):
    for axis in VOCAB:
        far, low, high = shift(s, axis, 2), shift(s, axis, 1), shift(s, axis, 3)
        s = pl.pallas_call(
            merge_kernel,
            out_shape=jax.ShapeDtypeStruct(s.shape, s.dtype),
            in_specs=[pl.BlockSpec(memory_space=pltpu.VMEM)] * 4,
            out_specs=pl.BlockSpec(memory_space=pltpu.VMEM),
            compiler_params=pltpu.CompilerParams(vmem_limit_bytes=2**20),
            name="merge",
        )(s, low, high, far)
    return s


def gather_rows(part):
    rows, cols = part.shape
    y = lax.axis_index("y")
    chip = jnp.zeros((2, 4, rows, cols), part.dtype)
    for dz, dy in ((1, 2), (0, 2), (1, 1), (1, 3), (0, 1), (0, 3), (1, 0), (0, 0)):
        piece = part
        if dz or dy:
            moves = [
                (z * 4 + j, ((z + dz) % 2) * 4 + (j + dy) % 4) for z in range(2) for j in range(4)
            ]
            piece = lax.ppermute(part, ("zl", "y"), moves)
        chip = lax.dynamic_update_slice(chip, piece[None, None], (dz, (y - dy) % 4, 0, 0))
    chip = chip.reshape(8 * rows, cols)
    return chip, shift(chip, "c", 1)


def local(hidden_rows, translator, final_gain, unembed, target_logits):
    row_count, feature_count = hidden_rows.shape
    col_count = translator.shape[1]
    first_col = lax.axis_index(VOCAB) * col_count
    zl, c = lax.axis_index("zl"), lax.axis_index("c")
    first, second = gather_unembed(unembed)
    own_inputs = lax.dynamic_slice_in_dim(hidden_rows, first_col, col_count, 1).astype(jnp.float32)
    own_part = (
        own_inputs + jnp.dot(hidden_rows, translator, preferred_element_type=jnp.float32)
    ).astype(jnp.bfloat16)
    translated = gather_translated(own_part)
    trans_values = translated.astype(jnp.float32)
    inv_rms = lax.rsqrt(jnp.mean(trans_values * trans_values, axis=1, keepdims=True) + EPSILON)
    normed = (trans_values * inv_rms * final_gain).astype(jnp.bfloat16)
    second[4], hidden_late = lax.optimization_barrier((second[4], hidden_rows))
    slices = lax.all_to_all(
        hidden_late.reshape(row_count, 2, 8, col_count), ("y", "c"), split_axis=2, concat_axis=0, tiled=True
    )
    target = target_logits.astype(jnp.float32)
    target_top = jnp.max(target, axis=1)
    target_off = target - target_top[:, None]
    target_exp = jnp.exp(target_off)
    target_total = jnp.sum(target_exp, axis=1)
    target_mean = jnp.sum(target_exp * target_off, axis=1)
    logits = forward(normed, first, second)
    model_top = jnp.max(logits, axis=1)
    model_off = logits - model_top[:, None]
    model_exp = jnp.exp(model_off)
    mine = jnp.stack(
        [
            model_top,
            jnp.sum(model_exp, axis=1),
            jnp.sum(model_exp * model_off, axis=1),
            target_top,
            target_total,
            target_mean,
            jnp.sum(target_exp * model_off, axis=1),
            jnp.zeros_like(model_top),
        ]
    )
    whole = merge(mine)
    model_sum, target_sum = whole[1], whole[4]
    row_kl = (
        (whole[5] - whole[6]) / target_sum - jnp.log(target_sum) + jnp.log(model_sum)
    )
    inner = (whole[2] / model_sum - whole[6] / target_sum) / (inv_rms[:, 0] * feature_count)
    prob_model = jnp.exp(logits - whole[0][:, None]) / model_sum[:, None]
    prob_target = jnp.exp(target - whole[3][:, None]) / target_sum[:, None]
    grad_logits = (prob_model - prob_target).astype(jnp.bfloat16)
    sums, moved = [], []
    for step, kz in enumerate((2, 1, 3, 0)):
        if step >= 2:
            grad_logits, sums[step - 2] = lax.optimization_barrier((grad_logits, sums[step - 2]))
            moved.append(shift(sums[step - 2], "zh", (2, 1)[step - 2]))
        blocks = list(backward(kz, grad_logits, first, second, col_count))
        if step == 1:
            blocks[3], slices = lax.optimization_barrier((blocks[3], slices))
            slices = slices.reshape(8 * row_count, 2, col_count)
            near = lax.dynamic_index_in_dim(slices, zl, 1, False)
            far = shift(lax.dynamic_index_in_dim(slices, 1 - zl, 1, False), "zl", 1)
        total = blocks[0]
        for kx in (2, 1, 3):
            total = total + shift(blocks[kx], "x", kx)
        sums.append(total)
    sums[2], moved[0] = lax.optimization_barrier((sums[2], moved[0]))
    moved.append(shift(sums[2], "zh", 3))
    sums[3], moved[1], far = lax.optimization_barrier((sums[3], moved[1], far))
    grad_cols = sums[3] + moved[0] + moved[1] + moved[2]
    slices = jnp.stack([near, far]).reshape(2, 4, 2, row_count, col_count)
    slices_own = lax.dynamic_index_in_dim(slices, c, 2, False).reshape(8 * row_count, col_count)
    slices_other = lax.dynamic_index_in_dim(slices, 1 - c, 2, False).reshape(8 * row_count, col_count)
    gain_cols = lax.dynamic_slice_in_dim(final_gain, first_col, col_count, 0)
    value_cols = own_part.astype(jnp.float32)
    scaled = grad_cols * gain_cols
    grad_translated = (inv_rms * scaled - value_cols * inv_rms**3 * inner[:, None]).astype(
        jnp.bfloat16
    )
    chip, other = gather_rows(grad_translated)
    over_rows = (((0,), (0,)), ((), ()))
    grad_translator = lax.dot_general(
        slices_own, chip, over_rows, preferred_element_type=jnp.float32
    )
    grad_translator, other = lax.optimization_barrier((grad_translator, other))
    grad_translator += lax.dot_general(
        slices_other, other, over_rows, preferred_element_type=jnp.float32
    )
    return (grad_translator, row_kl)


def solution(mesh):
    split = Mesh(mesh.devices.reshape(tuple(SIZES.values())), tuple(SIZES))
    return jax.shard_map(
        local,
        mesh=split,
        in_specs=(P(DP, None), P(None, VOCAB), P(), P(DP, VOCAB), P(DP, VOCAB)),
        out_specs=(P(DP, VOCAB), P(DP)),
        check_vma=False,
    )
```

```python
import functools

import jax
import jax.numpy as jnp
from jax import lax
from jax.experimental import pallas as pl
from jax.experimental.pallas import tpu as pltpu
from jax.sharding import Mesh, PartitionSpec as P

EPSILON = 1e-05
SIZES = {"zl": 2, "y": 4, "c": 2, "zh": 4, "x": 4}
DP = ("zl", "y", "c")
VOCAB = ("zh", "x")


def shift(value, axis, step):
    size = SIZES[axis]
    return lax.ppermute(value, axis, [(i, (i + step) % size) for i in range(size)])


def gather(part, unembed):
    rows, cols = part.shape
    zh, x = lax.axis_index("zh"), lax.axis_index("x")
    half = unembed.shape[0] // 2
    low, high = shift(unembed, "y", 1), shift(unembed, "y", 3)
    partner = shift(unembed, "zl", 1)
    got = jnp.zeros((rows, 4 * cols), part.dtype)
    for k in range(4):
        piece = shift(part, "zh", k) if k else part
        got = lax.dynamic_update_slice(got, piece, (0, ((zh - k) % 4) * cols))
    got, low, high = lax.optimization_barrier((got, low, high))
    far_top, far_end = shift(low[:half], "y", 1), shift(high[half:], "y", 3)
    partner_low, partner_high = shift(partner, "y", 1), shift(partner, "y", 3)
    whole = jnp.zeros((rows, 16 * cols), part.dtype)
    near = [got] + [shift(got, "x", k) for k in (1, 2, 3)]
    *near, far_top, far_end, partner_low, partner_high = lax.optimization_barrier(
        (*near, far_top, far_end, partner_low, partner_high)
    )
    last_top, last_end = shift(partner_low[:half], "y", 1), shift(partner_high[half:], "y", 3)
    pieces = []
    for value, *spot in (
        (unembed, 0, 0, 0),
        (low, 0, 1, 0),
        (high, 0, 3, 0),
        (far_top, 0, 2, 0),
        (far_end, 0, 2, half),
        (partner, 1, 0, 0),
        (partner_low, 1, 1, 0),
        (partner_high, 1, 3, 0),
        (last_top, 1, 2, 0),
        (last_end, 1, 2, half),
    ):
        dz, dy, row = spot
        pieces += [(value, (dz, dy, 0, row)), (shift(value, "c", 1), (dz, dy, 1, row))]
    for k in range(4):
        for z in range(4):
            whole = lax.dynamic_update_slice(
                whole, near[k][:, z * cols : (z + 1) * cols], (0, (z * 4 + (x - k) % 4) * cols)
            )
    return whole, pieces


def position():
    return jnp.stack([lax.axis_index(a) for a in SIZES]).astype(jnp.int32)


def piece_block(place, spot):
    dz, dy, dc, _ = spot
    zl = (place[0] + (2 - dz)) % 2
    y = (place[1] + (4 - dy)) % 4
    c = (place[2] + (2 - dc)) % 2
    return zl * 8 + y * 2 + c


def forward_kernel(heights, spots, block, place, normed, *refs):
    count = len(heights)
    pieces, out, held, sems = refs[:count], refs[count], refs[count + 1], refs[count + 2]
    copies, start = [], 0
    for p, height in enumerate(heights):
        copies.append(
            pltpu.make_async_copy(pieces[p], held.at[pl.ds(start, height)], sems.at[p])
        )
        copies[-1].start()
        start += height
    start = 0
    for p, height in enumerate(heights):
        copies[p].wait()
        first = piece_block(place, spots[p]) * block + spots[p][3]
        cols = normed[:, pl.ds(pl.multiple_of(first, 256), height)]
        term = jnp.dot(cols, held[pl.ds(start, height), :], preferred_element_type=jnp.float32)
        if p:
            out[...] += term
        else:
            out[...] = term
        start += height


def forward(normed, pieces, block):
    heights = [p[0].shape[0] for p in pieces]
    rows, cols = normed.shape[0], pieces[0][0].shape[1]
    spots = [p[1] for p in pieces]
    return pl.pallas_call(
        functools.partial(forward_kernel, heights, spots, block),
        out_shape=jax.ShapeDtypeStruct((rows, cols), jnp.float32),
        in_specs=[
            pl.BlockSpec(memory_space=pltpu.SMEM),
            pl.BlockSpec(memory_space=pltpu.VMEM),
        ]
        + [pl.BlockSpec(memory_space=pltpu.HBM)] * len(pieces),
        out_specs=pl.BlockSpec(memory_space=pltpu.VMEM),
        scratch_shapes=[
            pltpu.VMEM((sum(heights), cols), jnp.bfloat16),
            pltpu.SemaphoreType.DMA((len(pieces),)),
        ],
        compiler_params=pltpu.CompilerParams(vmem_limit_bytes=54 * 2**20),
        cost_estimate=pl.CostEstimate(
            flops=2 * rows * cols * sum(heights), bytes_accessed=2 * cols * sum(heights), transcendentals=0
        ),
        name="forward",
    )(position(), normed, *[p[0] for p in pieces])


def backward_kernel(kz, spots, place, grad, *refs):
    count = len(spots)
    pieces, outs, held, sems = refs[:count], refs[count : count + 4], refs[count + 4], refs[count + 5]
    order = (2, 1, 3, 0)
    for kx in order:
        wanted = ((place[3] + kz) % 4) * 4 + (place[4] + kx) % 4
        for piece, spot in zip(pieces, spots):

            @pl.when(piece_block(place, spot) == wanted)
            def _():
                pltpu.make_async_copy(
                    piece, held.at[kx, pl.ds(spot[3], piece.shape[0])], sems.at[kx]
                ).start()

    for kx in order:
        pltpu.make_async_copy(pieces[0], held.at[kx], sems.at[kx]).wait()
        outs[kx][...] = lax.dot_general(
            grad[...], held[kx], (((1,), (1,)), ((), ())), preferred_element_type=jnp.float32
        )


def backward(kz, grad, pieces, block):
    rows, cols = grad.shape
    return pl.pallas_call(
        functools.partial(backward_kernel, kz, [p[1] for p in pieces]),
        out_shape=[jax.ShapeDtypeStruct((rows, block), jnp.float32)] * 4,
        in_specs=[
            pl.BlockSpec(memory_space=pltpu.SMEM),
            pl.BlockSpec(memory_space=pltpu.VMEM),
        ]
        + [pl.BlockSpec(memory_space=pltpu.HBM)] * len(pieces),
        out_specs=[pl.BlockSpec(memory_space=pltpu.VMEM)] * 4,
        scratch_shapes=[
            pltpu.VMEM((4, block, cols), jnp.bfloat16),
            pltpu.SemaphoreType.DMA((4,)),
        ],
        compiler_params=pltpu.CompilerParams(vmem_limit_bytes=50 * 2**20),
        cost_estimate=pl.CostEstimate(
            flops=8 * rows * cols * block,
            bytes_accessed=8 * cols * block + 16 * rows * block,
            transcendentals=0,
        ),
        name="backward",
    )(position(), grad, *[p[0] for p in pieces])


def merge_kernel(a, b, c, d, out):
    groups = (a, b, c, d)
    top = jnp.maximum(jnp.maximum(a[0:1], b[0:1]), jnp.maximum(c[0:1], d[0:1]))
    ttop = jnp.maximum(jnp.maximum(a[3:4], b[3:4]), jnp.maximum(c[3:4], d[3:4]))
    sums = [jnp.zeros_like(top) for _ in range(5)]
    for v in groups:
        dm, dt = v[0:1] - top, v[3:4] - ttop
        em, et = jnp.exp(dm), jnp.exp(dt)
        sums[0] += em * v[1:2]
        sums[1] += em * (v[2:3] + dm * v[1:2])
        sums[2] += et * v[4:5]
        sums[3] += et * (v[5:6] + dt * v[4:5])
        sums[4] += et * (v[6:7] + dm * v[4:5])
    for row, value in enumerate((top, sums[0], sums[1], ttop, sums[2], sums[3], sums[4], top)):
        out[row : row + 1] = value


def merge(s):
    for axis in VOCAB:
        far, low, high = shift(s, axis, 2), shift(s, axis, 1), shift(s, axis, 3)
        s = pl.pallas_call(
            merge_kernel,
            out_shape=jax.ShapeDtypeStruct(s.shape, s.dtype),
            in_specs=[pl.BlockSpec(memory_space=pltpu.VMEM)] * 4,
            out_specs=pl.BlockSpec(memory_space=pltpu.VMEM),
            compiler_params=pltpu.CompilerParams(vmem_limit_bytes=2**20),
            name="merge",
        )(s, low, high, far)
    return s


def gather_rows(part):
    rows, cols = part.shape
    y = lax.axis_index("y")
    chip = jnp.zeros((4, 2, rows, cols), part.dtype)
    for dz, dy in ((1, 2), (0, 2), (1, 1), (1, 3), (0, 1), (0, 3), (1, 0), (0, 0)):
        piece = part
        if dz or dy:
            moves = [
                (z * 4 + j, ((z + dz) % 2) * 4 + (j + dy) % 4) for z in range(2) for j in range(4)
            ]
            piece = lax.ppermute(part, ("zl", "y"), moves)
        chip = lax.dynamic_update_slice(chip, piece[None, None], ((y - dy) % 4, dz, 0, 0))
    chip = chip.reshape(8 * rows, cols)
    return chip, shift(chip, "c", 1)


def local(hidden_rows, translator, final_gain, unembed, target_logits):
    row_count, feature_count = hidden_rows.shape
    col_count = translator.shape[1]
    first_col = lax.axis_index(VOCAB) * col_count
    zl, c = lax.axis_index("zl"), lax.axis_index("c")
    own_inputs = lax.dynamic_slice_in_dim(hidden_rows, first_col, col_count, 1).astype(jnp.float32)
    own_part = (
        own_inputs + jnp.dot(hidden_rows, translator, preferred_element_type=jnp.float32)
    ).astype(jnp.bfloat16)
    translated, pieces = gather(own_part, unembed)
    trans_values = translated.astype(jnp.float32)
    inv_rms = lax.rsqrt(jnp.mean(trans_values * trans_values, axis=1, keepdims=True) + EPSILON)
    normed = (trans_values * inv_rms * final_gain).astype(jnp.bfloat16)
    half = feature_count // 2
    hidden_near = lax.dynamic_slice_in_dim(hidden_rows, zl * half, half, 1)
    hidden_far = lax.dynamic_slice_in_dim(hidden_rows, (1 - zl) * half, half, 1)
    last, last_spot = pieces[18]
    last, hidden_near, hidden_far = lax.optimization_barrier((last, hidden_near, hidden_far))
    pieces[18] = (last, last_spot)
    hidden_far = shift(hidden_far, "zl", 1)
    target = target_logits.astype(jnp.float32)
    target_top = jnp.max(target, axis=1)
    target_off = target - target_top[:, None]
    target_exp = jnp.exp(target_off)
    target_total = jnp.sum(target_exp, axis=1)
    target_mean = jnp.sum(target_exp * target_off, axis=1)
    logits = forward(normed, pieces, unembed.shape[0])
    model_top = jnp.max(logits, axis=1)
    model_off = logits - model_top[:, None]
    model_exp = jnp.exp(model_off)
    mine = jnp.stack(
        [
            model_top,
            jnp.sum(model_exp, axis=1),
            jnp.sum(model_exp * model_off, axis=1),
            target_top,
            target_total,
            target_mean,
            jnp.sum(target_exp * model_off, axis=1),
            jnp.zeros_like(model_top),
        ]
    )
    whole = merge(mine)
    model_sum, target_sum = whole[1], whole[4]
    row_kl = (
        (whole[5] - whole[6]) / target_sum - jnp.log(target_sum) + jnp.log(model_sum)
    )
    inner = (whole[2] / model_sum - whole[6] / target_sum) / (inv_rms[:, 0] * feature_count)
    prob_model = jnp.exp(logits - whole[0][:, None]) / model_sum[:, None]
    prob_target = jnp.exp(target - whole[3][:, None]) / target_sum[:, None]
    grad_logits = (prob_model - prob_target).astype(jnp.bfloat16)
    sums, moved = [], []
    for step, kz in enumerate((2, 1, 3, 0)):
        if step >= 2:
            grad_logits, sums[step - 2] = lax.optimization_barrier((grad_logits, sums[step - 2]))
            moved.append(shift(sums[step - 2], "zh", (2, 1)[step - 2]))
        blocks = list(backward(kz, grad_logits, pieces, col_count))
        if step == 1:
            blocks[3], hidden_near, hidden_far = lax.optimization_barrier(
                (blocks[3], hidden_near, hidden_far)
            )
            slices = lax.all_to_all(
                jnp.concatenate([hidden_near, hidden_far], axis=0),
                ("y", "c"),
                split_axis=1,
                concat_axis=0,
                tiled=True,
            )
        total = blocks[0]
        for kx in (2, 1, 3):
            total = total + shift(blocks[kx], "x", kx)
        sums.append(total)
    moved.append(shift(sums[2], "zh", 3))
    sums[3], moved[1], slices = lax.optimization_barrier((sums[3], moved[1], slices))
    grad_cols = sums[3] + moved[0] + moved[1] + moved[2]
    slices = slices.reshape(4, 2, 2 * row_count, col_count)
    slices_own = lax.dynamic_index_in_dim(slices, c, 1, False).reshape(8 * row_count, col_count)
    slices_other = lax.dynamic_index_in_dim(slices, 1 - c, 1, False).reshape(8 * row_count, col_count)
    gain_cols = lax.dynamic_slice_in_dim(final_gain, first_col, col_count, 0)
    value_cols = own_part.astype(jnp.float32)
    scaled = grad_cols * gain_cols
    grad_translated = (inv_rms * scaled - value_cols * inv_rms**3 * inner[:, None]).astype(
        jnp.bfloat16
    )
    chip, other = gather_rows(grad_translated)
    over_rows = (((0,), (0,)), ((), ()))
    grad_translator = lax.dot_general(
        slices_own, chip, over_rows, preferred_element_type=jnp.float32
    )
    grad_translator, other = lax.optimization_barrier((grad_translator, other))
    grad_translator += lax.dot_general(
        slices_other, other, over_rows, preferred_element_type=jnp.float32
    )
    return (grad_translator, row_kl)


def solution(mesh):
    split = Mesh(mesh.devices.reshape(tuple(SIZES.values())), tuple(SIZES))
    return jax.shard_map(
        local,
        mesh=split,
        in_specs=(P(DP, None), P(None, VOCAB), P(), P(DP, VOCAB), P(DP, VOCAB)),
        out_specs=(P(DP, VOCAB), P(DP)),
        check_vma=False,
    )
```

```python
import functools

import jax
import jax.numpy as jnp
from jax import lax
from jax.experimental import pallas as pl
from jax.experimental.pallas import tpu as pltpu
from jax.sharding import Mesh, PartitionSpec as P

EPSILON = 1e-05
SIZES = {"zl": 2, "y": 4, "c": 2, "zh": 4, "x": 4}
DP = ("zl", "y", "c")
VOCAB = ("zh", "x")


def shift(value, axis, step):
    size = SIZES[axis]
    return lax.ppermute(value, axis, [(i, (i + step) % size) for i in range(size)])


def gather(part, unembed):
    half = unembed.shape[0] // 2
    low, high = shift(unembed, "y", 1), shift(unembed, "y", 3)
    partner = shift(unembed, "zl", 1)
    near = lax.all_gather(part, VOCAB, axis=1, tiled=True)
    far_top, far_end = shift(low[:half], "y", 1), shift(high[half:], "y", 3)
    partner_low, partner_high = shift(partner, "y", 1), shift(partner, "y", 3)
    last_top, last_end = shift(partner_low[:half], "y", 1), shift(partner_high[half:], "y", 3)
    pieces = []
    for value, *spot in (
        (unembed, 0, 0, 0),
        (low, 0, 1, 0),
        (high, 0, 3, 0),
        (far_top, 0, 2, 0),
        (far_end, 0, 2, half),
        (partner, 1, 0, 0),
        (partner_low, 1, 1, 0),
        (partner_high, 1, 3, 0),
        (last_top, 1, 2, 0),
        (last_end, 1, 2, half),
    ):
        dz, dy, row = spot
        pieces += [(value, (dz, dy, 0, row)), (shift(value, "c", 1), (dz, dy, 1, row))]
    return near, pieces


def position():
    return jnp.stack([lax.axis_index(a) for a in SIZES]).astype(jnp.int32)


def normalize_kernel(gain, near, normed, inverse):
    step = normed.shape[1] // 16
    total = jnp.zeros((normed.shape[0], 1), jnp.float32)
    for k in range(16):
        wide = near[:, pl.ds(k * step, step)].astype(jnp.float32)
        total += jnp.sum(wide * wide, axis=1, keepdims=True)
    inv_rms = lax.rsqrt(total / normed.shape[1] + EPSILON)
    inverse[...] = jnp.broadcast_to(inv_rms, inverse.shape)
    for k in range(16):
        at = pl.ds(k * step, step)
        wide = near[:, at].astype(jnp.float32)
        normed[:, at] = (wide * inv_rms * gain[:, at]).astype(normed.dtype)


def normalize(near, gain):
    rows, features = near.shape
    return pl.pallas_call(
        normalize_kernel,
        out_shape=[
            jax.ShapeDtypeStruct((rows, features), near.dtype),
            jax.ShapeDtypeStruct((rows, 128), jnp.float32),
        ],
        in_specs=[pl.BlockSpec(memory_space=pltpu.VMEM)] * 2,
        out_specs=[pl.BlockSpec(memory_space=pltpu.VMEM)] * 2,
        compiler_params=pltpu.CompilerParams(vmem_limit_bytes=24 * 2**20),
        cost_estimate=pl.CostEstimate(
            flops=6 * rows * features, bytes_accessed=4 * rows * features, transcendentals=rows
        ),
        name="normalize",
    )(gain[None], near)


def piece_block(place, spot):
    dz, dy, dc, _ = spot
    zl = (place[0] + (2 - dz)) % 2
    y = (place[1] + (4 - dy)) % 4
    c = (place[2] + (2 - dc)) % 2
    return zl * 8 + y * 2 + c


def forward_kernel(heights, spots, block, place, normed, *refs):
    count = len(heights)
    pieces, out, held, sems = refs[:count], refs[count], refs[count + 1], refs[count + 2]
    copies, start = [], 0
    for p, height in enumerate(heights):
        copies.append(
            pltpu.make_async_copy(pieces[p], held.at[pl.ds(start, height)], sems.at[p])
        )
        copies[-1].start()
        start += height
    start = 0
    for p, height in enumerate(heights):
        copies[p].wait()
        first = piece_block(place, spots[p]) * block + spots[p][3]
        cols = normed[:, pl.ds(pl.multiple_of(first, 256), height)]
        term = jnp.dot(cols, held[pl.ds(start, height), :], preferred_element_type=jnp.float32)
        if p:
            out[...] += term
        else:
            out[...] = term
        start += height


def forward(normed, pieces, block):
    heights = [p[0].shape[0] for p in pieces]
    rows, cols = normed.shape[0], pieces[0][0].shape[1]
    spots = [p[1] for p in pieces]
    return pl.pallas_call(
        functools.partial(forward_kernel, heights, spots, block),
        out_shape=jax.ShapeDtypeStruct((rows, cols), jnp.float32),
        in_specs=[
            pl.BlockSpec(memory_space=pltpu.SMEM),
            pl.BlockSpec(memory_space=pltpu.VMEM),
        ]
        + [pl.BlockSpec(memory_space=pltpu.HBM)] * len(pieces),
        out_specs=pl.BlockSpec(memory_space=pltpu.VMEM),
        scratch_shapes=[
            pltpu.VMEM((sum(heights), cols), jnp.bfloat16),
            pltpu.SemaphoreType.DMA((len(pieces),)),
        ],
        compiler_params=pltpu.CompilerParams(vmem_limit_bytes=54 * 2**20),
        cost_estimate=pl.CostEstimate(
            flops=2 * rows * cols * sum(heights), bytes_accessed=2 * cols * sum(heights), transcendentals=0
        ),
        name="forward",
    )(position(), normed, *[p[0] for p in pieces])


def backward_kernel(kz, spots, place, grad, *refs):
    count = len(spots)
    pieces, outs, held, sems = refs[:count], refs[count : count + 4], refs[count + 4], refs[count + 5]
    order = (2, 1, 3, 0)
    for kx in order:
        wanted = ((place[3] + kz) % 4) * 4 + (place[4] + kx) % 4
        for piece, spot in zip(pieces, spots):

            @pl.when(piece_block(place, spot) == wanted)
            def _():
                pltpu.make_async_copy(
                    piece, held.at[kx, pl.ds(spot[3], piece.shape[0])], sems.at[kx]
                ).start()

    for kx in order:
        pltpu.make_async_copy(pieces[0], held.at[kx], sems.at[kx]).wait()
        outs[kx][...] = lax.dot_general(
            grad[...], held[kx], (((1,), (1,)), ((), ())), preferred_element_type=jnp.float32
        )


def backward(kz, grad, pieces, block):
    rows, cols = grad.shape
    return pl.pallas_call(
        functools.partial(backward_kernel, kz, [p[1] for p in pieces]),
        out_shape=[jax.ShapeDtypeStruct((rows, block), jnp.float32)] * 4,
        in_specs=[
            pl.BlockSpec(memory_space=pltpu.SMEM),
            pl.BlockSpec(memory_space=pltpu.VMEM),
        ]
        + [pl.BlockSpec(memory_space=pltpu.HBM)] * len(pieces),
        out_specs=[pl.BlockSpec(memory_space=pltpu.VMEM)] * 4,
        scratch_shapes=[
            pltpu.VMEM((4, block, cols), jnp.bfloat16),
            pltpu.SemaphoreType.DMA((4,)),
        ],
        compiler_params=pltpu.CompilerParams(vmem_limit_bytes=50 * 2**20),
        cost_estimate=pl.CostEstimate(
            flops=8 * rows * cols * block,
            bytes_accessed=8 * cols * block + 16 * rows * block,
            transcendentals=0,
        ),
        name="backward",
    )(position(), grad, *[p[0] for p in pieces])


def merge_kernel(a, b, c, d, out):
    groups = (a, b, c, d)
    top = jnp.maximum(jnp.maximum(a[0:1], b[0:1]), jnp.maximum(c[0:1], d[0:1]))
    ttop = jnp.maximum(jnp.maximum(a[3:4], b[3:4]), jnp.maximum(c[3:4], d[3:4]))
    sums = [jnp.zeros_like(top) for _ in range(5)]
    for v in groups:
        dm, dt = v[0:1] - top, v[3:4] - ttop
        em, et = jnp.exp(dm), jnp.exp(dt)
        sums[0] += em * v[1:2]
        sums[1] += em * (v[2:3] + dm * v[1:2])
        sums[2] += et * v[4:5]
        sums[3] += et * (v[5:6] + dt * v[4:5])
        sums[4] += et * (v[6:7] + dm * v[4:5])
    for row, value in enumerate((top, sums[0], sums[1], ttop, sums[2], sums[3], sums[4], top)):
        out[row : row + 1] = value


def merge(s):
    for axis in VOCAB:
        far, low, high = shift(s, axis, 2), shift(s, axis, 1), shift(s, axis, 3)
        s = pl.pallas_call(
            merge_kernel,
            out_shape=jax.ShapeDtypeStruct(s.shape, s.dtype),
            in_specs=[pl.BlockSpec(memory_space=pltpu.VMEM)] * 4,
            out_specs=pl.BlockSpec(memory_space=pltpu.VMEM),
            compiler_params=pltpu.CompilerParams(vmem_limit_bytes=2**20),
            name="merge",
        )(s, low, high, far)
    return s


def gather_rows(part):
    rows, cols = part.shape
    y = lax.axis_index("y")
    chip = jnp.zeros((4, 2, rows, cols), part.dtype)
    for dz, dy in ((1, 2), (0, 2), (1, 1), (1, 3), (0, 1), (0, 3), (1, 0), (0, 0)):
        piece = part
        if dz or dy:
            moves = [
                (z * 4 + j, ((z + dz) % 2) * 4 + (j + dy) % 4) for z in range(2) for j in range(4)
            ]
            piece = lax.ppermute(part, ("zl", "y"), moves)
        chip = lax.dynamic_update_slice(chip, piece[None, None], ((y - dy) % 4, dz, 0, 0))
    chip = chip.reshape(8 * rows, cols)
    return chip, shift(chip, "c", 1)


def local(hidden_rows, translator, final_gain, unembed, target_logits):
    row_count, feature_count = hidden_rows.shape
    col_count = translator.shape[1]
    first_col = lax.axis_index(VOCAB) * col_count
    zl, c = lax.axis_index("zl"), lax.axis_index("c")
    own_inputs = lax.dynamic_slice_in_dim(hidden_rows, first_col, col_count, 1).astype(jnp.float32)
    own_part = (
        own_inputs + jnp.dot(hidden_rows, translator, preferred_element_type=jnp.float32)
    ).astype(jnp.bfloat16)
    near, pieces = gather(own_part, unembed)
    normed, inverse = normalize(near, final_gain)
    inv_rms = inverse[:, :1]
    half = feature_count // 2
    hidden_near = lax.dynamic_slice_in_dim(hidden_rows, zl * half, half, 1)
    hidden_far = lax.dynamic_slice_in_dim(hidden_rows, (1 - zl) * half, half, 1)
    last, last_spot = pieces[18]
    last, hidden_near, hidden_far = lax.optimization_barrier((last, hidden_near, hidden_far))
    pieces[18] = (last, last_spot)
    hidden_far = shift(hidden_far, "zl", 1)
    target = target_logits.astype(jnp.float32)
    target_top = jnp.max(target, axis=1)
    target_off = target - target_top[:, None]
    target_exp = jnp.exp(target_off)
    target_total = jnp.sum(target_exp, axis=1)
    target_mean = jnp.sum(target_exp * target_off, axis=1)
    logits = forward(normed, pieces, unembed.shape[0])
    model_top = jnp.max(logits, axis=1)
    model_off = logits - model_top[:, None]
    model_exp = jnp.exp(model_off)
    mine = jnp.stack(
        [
            model_top,
            jnp.sum(model_exp, axis=1),
            jnp.sum(model_exp * model_off, axis=1),
            target_top,
            target_total,
            target_mean,
            jnp.sum(target_exp * model_off, axis=1),
            jnp.zeros_like(model_top),
        ]
    )
    whole = merge(mine)
    model_sum, target_sum = whole[1], whole[4]
    row_kl = (
        (whole[5] - whole[6]) / target_sum - jnp.log(target_sum) + jnp.log(model_sum)
    )
    inner = (whole[2] / model_sum - whole[6] / target_sum) / (inv_rms[:, 0] * feature_count)
    prob_model = jnp.exp(logits - whole[0][:, None]) / model_sum[:, None]
    prob_target = jnp.exp(target - whole[3][:, None]) / target_sum[:, None]
    grad_logits = (prob_model - prob_target).astype(jnp.bfloat16)
    hidden_both = jnp.concatenate([hidden_near, hidden_far], axis=0)
    hidden_both = hidden_both.reshape(2 * row_count, 8, col_count).transpose(1, 0, 2)
    grad_logits, hidden_both = lax.optimization_barrier((grad_logits, hidden_both))
    sums, moved = [], []
    for step, kz in enumerate((2, 1, 3, 0)):
        if step >= 2:
            grad_logits, sums[step - 2] = lax.optimization_barrier((grad_logits, sums[step - 2]))
            moved.append(shift(sums[step - 2], "zh", (2, 1)[step - 2]))
        blocks = list(backward(kz, grad_logits, pieces, col_count))
        if step == 1:
            blocks[3], hidden_both = lax.optimization_barrier((blocks[3], hidden_both))
            slices = lax.all_to_all(hidden_both, ("y", "c"), split_axis=0, concat_axis=0, tiled=True)
        total = blocks[0]
        for kx in (2, 1, 3):
            total = total + shift(blocks[kx], "x", kx)
        sums.append(total)
    moved.append(shift(sums[2], "zh", 3))
    sums[3], moved[1], slices = lax.optimization_barrier((sums[3], moved[1], slices))
    grad_cols = sums[3] + moved[0] + moved[1] + moved[2]
    slices = slices.reshape(4, 2, 2 * row_count, col_count)
    slices_own = lax.dynamic_index_in_dim(slices, c, 1, False).reshape(8 * row_count, col_count)
    slices_other = lax.dynamic_index_in_dim(slices, 1 - c, 1, False).reshape(8 * row_count, col_count)
    gain_cols = lax.dynamic_slice_in_dim(final_gain, first_col, col_count, 0)
    value_cols = own_part.astype(jnp.float32)
    scaled = grad_cols * gain_cols
    grad_translated = (inv_rms * scaled - value_cols * inv_rms**3 * inner[:, None]).astype(
        jnp.bfloat16
    )
    chip, other = gather_rows(grad_translated)
    over_rows = (((0,), (0,)), ((), ()))
    grad_translator = lax.dot_general(
        slices_own, chip, over_rows, preferred_element_type=jnp.float32
    )
    grad_translator, other = lax.optimization_barrier((grad_translator, other))
    grad_translator += lax.dot_general(
        slices_other, other, over_rows, preferred_element_type=jnp.float32
    )
    return (grad_translator, row_kl)


def solution(mesh):
    split = Mesh(mesh.devices.reshape(tuple(SIZES.values())), tuple(SIZES))
    return jax.shard_map(
        local,
        mesh=split,
        in_specs=(P(DP, None), P(None, VOCAB), P(), P(DP, VOCAB), P(DP, VOCAB)),
        out_specs=(P(DP, VOCAB), P(DP)),
        check_vma=False,
    )
```

```python
import functools

import jax
import jax.numpy as jnp
from jax import lax
from jax.experimental import pallas as pl
from jax.experimental.pallas import tpu as pltpu
from jax.sharding import Mesh, PartitionSpec as P

EPSILON = 1e-05
SIZES = {"zl": 2, "y": 4, "c": 2, "zh": 4, "x": 4}
DP = ("zl", "y", "c")
VOCAB = ("zh", "x")


def shift(value, axis, step):
    size = SIZES[axis]
    return lax.ppermute(value, axis, [(i, (i + step) % size) for i in range(size)])


def gather(part, unembed):
    half = unembed.shape[0] // 2
    low, high = shift(unembed, "y", 1), shift(unembed, "y", 3)
    partner = shift(unembed, "zl", 1)
    near = lax.all_gather(part, VOCAB, axis=1, tiled=True)
    far_top, far_end = shift(low[:half], "y", 1), shift(high[half:], "y", 3)
    partner_low, partner_high = shift(partner, "y", 1), shift(partner, "y", 3)
    last_top, last_end = shift(far_top, "zl", 1), shift(far_end, "zl", 1)
    unembed, low, high, far_top, far_end, partner, partner_low, partner_high = lax.optimization_barrier(
        (unembed, low, high, far_top, far_end, partner, partner_low, partner_high)
    )
    pieces = []
    for value, *spot in (
        (unembed, 0, 0, 0),
        (low, 0, 1, 0),
        (high, 0, 3, 0),
        (far_top, 0, 2, 0),
        (far_end, 0, 2, half),
        (partner, 1, 0, 0),
        (partner_low, 1, 1, 0),
        (partner_high, 1, 3, 0),
        (last_top, 1, 2, 0),
        (last_end, 1, 2, half),
    ):
        dz, dy, row = spot
        pieces += [(value, (dz, dy, 0, row)), (shift(value, "c", 1), (dz, dy, 1, row))]
    return near, pieces


def position():
    return jnp.stack([lax.axis_index(a) for a in SIZES]).astype(jnp.int32)


def normalize_kernel(gain, near, normed, inverse):
    step = normed.shape[1] // 16
    total = jnp.zeros((normed.shape[0], 1), jnp.float32)
    for k in range(16):
        wide = near[:, pl.ds(k * step, step)].astype(jnp.float32)
        total += jnp.sum(wide * wide, axis=1, keepdims=True)
    inv_rms = lax.rsqrt(total / normed.shape[1] + EPSILON)
    inverse[...] = jnp.broadcast_to(inv_rms, inverse.shape)
    for k in range(16):
        at = pl.ds(k * step, step)
        wide = near[:, at].astype(jnp.float32)
        normed[:, at] = (wide * inv_rms * gain[:, at]).astype(normed.dtype)


def normalize(near, gain):
    rows, features = near.shape
    return pl.pallas_call(
        normalize_kernel,
        out_shape=[
            jax.ShapeDtypeStruct((rows, features), near.dtype),
            jax.ShapeDtypeStruct((rows, 128), jnp.float32),
        ],
        in_specs=[pl.BlockSpec(memory_space=pltpu.VMEM)] * 2,
        out_specs=[pl.BlockSpec(memory_space=pltpu.VMEM)] * 2,
        compiler_params=pltpu.CompilerParams(vmem_limit_bytes=24 * 2**20),
        cost_estimate=pl.CostEstimate(
            flops=6 * rows * features, bytes_accessed=4 * rows * features, transcendentals=rows
        ),
        name="normalize",
    )(gain[None], near)


def piece_block(place, spot):
    dz, dy, dc, _ = spot
    zl = (place[0] + (2 - dz)) % 2
    y = (place[1] + (4 - dy)) % 4
    c = (place[2] + (2 - dc)) % 2
    return zl * 8 + y * 2 + c


def forward_kernel(heights, spots, block, place, normed, *refs):
    count = len(heights)
    pieces, out, held, sems = refs[:count], refs[count], refs[count + 1], refs[count + 2]
    copies, start = [], 0
    for p, height in enumerate(heights):
        copies.append(
            pltpu.make_async_copy(pieces[p], held.at[pl.ds(start, height)], sems.at[p])
        )
        copies[-1].start()
        start += height
    start = 0
    for p, height in enumerate(heights):
        copies[p].wait()
        first = piece_block(place, spots[p]) * block + spots[p][3]
        cols = normed[:, pl.ds(pl.multiple_of(first, 256), height)]
        term = jnp.dot(cols, held[pl.ds(start, height), :], preferred_element_type=jnp.float32)
        if p:
            out[...] += term
        else:
            out[...] = term
        start += height


def forward(normed, pieces, block):
    heights = [p[0].shape[0] for p in pieces]
    rows, cols = normed.shape[0], pieces[0][0].shape[1]
    spots = [p[1] for p in pieces]
    return pl.pallas_call(
        functools.partial(forward_kernel, heights, spots, block),
        out_shape=jax.ShapeDtypeStruct((rows, cols), jnp.float32),
        in_specs=[
            pl.BlockSpec(memory_space=pltpu.SMEM),
            pl.BlockSpec(memory_space=pltpu.VMEM),
        ]
        + [pl.BlockSpec(memory_space=pltpu.HBM)] * len(pieces),
        out_specs=pl.BlockSpec(memory_space=pltpu.VMEM),
        scratch_shapes=[
            pltpu.VMEM((sum(heights), cols), jnp.bfloat16),
            pltpu.SemaphoreType.DMA((len(pieces),)),
        ],
        compiler_params=pltpu.CompilerParams(vmem_limit_bytes=54 * 2**20),
        cost_estimate=pl.CostEstimate(
            flops=2 * rows * cols * sum(heights), bytes_accessed=2 * cols * sum(heights), transcendentals=0
        ),
        name="forward",
    )(position(), normed, *[p[0] for p in pieces])


def backward_kernel(kz, spots, place, grad, *refs):
    count = len(spots)
    pieces, outs, held, sems = refs[:count], refs[count : count + 4], refs[count + 4], refs[count + 5]
    order = (2, 1, 3, 0)
    for kx in order:
        wanted = ((place[3] + kz) % 4) * 4 + (place[4] + kx) % 4
        for piece, spot in zip(pieces, spots):

            @pl.when(piece_block(place, spot) == wanted)
            def _():
                pltpu.make_async_copy(
                    piece, held.at[kx, pl.ds(spot[3], piece.shape[0])], sems.at[kx]
                ).start()

    for kx in order:
        pltpu.make_async_copy(pieces[0], held.at[kx], sems.at[kx]).wait()
        outs[kx][...] = lax.dot_general(
            grad[...], held[kx], (((1,), (1,)), ((), ())), preferred_element_type=jnp.float32
        )


def backward(kz, grad, pieces, block):
    rows, cols = grad.shape
    return pl.pallas_call(
        functools.partial(backward_kernel, kz, [p[1] for p in pieces]),
        out_shape=[jax.ShapeDtypeStruct((rows, block), jnp.float32)] * 4,
        in_specs=[
            pl.BlockSpec(memory_space=pltpu.SMEM),
            pl.BlockSpec(memory_space=pltpu.VMEM),
        ]
        + [pl.BlockSpec(memory_space=pltpu.HBM)] * len(pieces),
        out_specs=[pl.BlockSpec(memory_space=pltpu.VMEM)] * 4,
        scratch_shapes=[
            pltpu.VMEM((4, block, cols), jnp.bfloat16),
            pltpu.SemaphoreType.DMA((4,)),
        ],
        compiler_params=pltpu.CompilerParams(vmem_limit_bytes=50 * 2**20),
        cost_estimate=pl.CostEstimate(
            flops=8 * rows * cols * block,
            bytes_accessed=8 * cols * block + 16 * rows * block,
            transcendentals=0,
        ),
        name="backward",
    )(position(), grad, *[p[0] for p in pieces])


def merge_kernel(a, b, c, d, out):
    groups = (a, b, c, d)
    top = jnp.maximum(jnp.maximum(a[0:1], b[0:1]), jnp.maximum(c[0:1], d[0:1]))
    ttop = jnp.maximum(jnp.maximum(a[3:4], b[3:4]), jnp.maximum(c[3:4], d[3:4]))
    sums = [jnp.zeros_like(top) for _ in range(5)]
    for v in groups:
        dm, dt = v[0:1] - top, v[3:4] - ttop
        em, et = jnp.exp(dm), jnp.exp(dt)
        sums[0] += em * v[1:2]
        sums[1] += em * (v[2:3] + dm * v[1:2])
        sums[2] += et * v[4:5]
        sums[3] += et * (v[5:6] + dt * v[4:5])
        sums[4] += et * (v[6:7] + dm * v[4:5])
    for row, value in enumerate((top, sums[0], sums[1], ttop, sums[2], sums[3], sums[4], top)):
        out[row : row + 1] = value


def merge(s):
    for axis in VOCAB:
        far, low, high = shift(s, axis, 2), shift(s, axis, 1), shift(s, axis, 3)
        s = pl.pallas_call(
            merge_kernel,
            out_shape=jax.ShapeDtypeStruct(s.shape, s.dtype),
            in_specs=[pl.BlockSpec(memory_space=pltpu.VMEM)] * 4,
            out_specs=pl.BlockSpec(memory_space=pltpu.VMEM),
            compiler_params=pltpu.CompilerParams(vmem_limit_bytes=2**20),
            name="merge",
        )(s, low, high, far)
    return s


def gather_rows(part):
    rows, cols = part.shape
    y = lax.axis_index("y")
    chip = jnp.zeros((2, 4, rows, cols), part.dtype)
    for dz, dy in ((1, 2), (0, 2), (1, 1), (1, 3), (0, 1), (0, 3), (1, 0), (0, 0)):
        piece = part
        if dz or dy:
            moves = [
                (z * 4 + j, ((z + dz) % 2) * 4 + (j + dy) % 4) for z in range(2) for j in range(4)
            ]
            piece = lax.ppermute(part, ("zl", "y"), moves)
        chip = lax.dynamic_update_slice(chip, piece[None, None], (dz, (y - dy) % 4, 0, 0))
    chip = chip.reshape(8 * rows, cols)
    return chip, shift(chip, "c", 1)


def local(hidden_rows, translator, final_gain, unembed, target_logits):
    row_count, feature_count = hidden_rows.shape
    col_count = translator.shape[1]
    first_col = lax.axis_index(VOCAB) * col_count
    zl, c = lax.axis_index("zl"), lax.axis_index("c")
    own_inputs = lax.dynamic_slice_in_dim(hidden_rows, first_col, col_count, 1).astype(jnp.float32)
    own_part = (
        own_inputs + jnp.dot(hidden_rows, translator, preferred_element_type=jnp.float32)
    ).astype(jnp.bfloat16)
    near, pieces = gather(own_part, unembed)
    normed, inverse = normalize(near, final_gain)
    inv_rms = inverse[:, :1]
    hidden_blocks = hidden_rows.reshape(row_count, 2, 8, col_count).transpose(2, 0, 1, 3)
    hidden_blocks = hidden_blocks.reshape(8, row_count, 2 * col_count)
    other, other_spot = pieces[11]
    other, hidden_blocks = lax.optimization_barrier((other, hidden_blocks))
    pieces[11] = (other, other_spot)
    slices = lax.all_to_all(hidden_blocks, ("y", "c"), split_axis=0, concat_axis=0, tiled=True)
    target = target_logits.astype(jnp.float32)
    target_top = jnp.max(target, axis=1)
    target_off = target - target_top[:, None]
    target_exp = jnp.exp(target_off)
    target_total = jnp.sum(target_exp, axis=1)
    target_mean = jnp.sum(target_exp * target_off, axis=1)
    logits = forward(normed, pieces, unembed.shape[0])
    model_top = jnp.max(logits, axis=1)
    model_off = logits - model_top[:, None]
    model_exp = jnp.exp(model_off)
    mine = jnp.stack(
        [
            model_top,
            jnp.sum(model_exp, axis=1),
            jnp.sum(model_exp * model_off, axis=1),
            target_top,
            target_total,
            target_mean,
            jnp.sum(target_exp * model_off, axis=1),
            jnp.zeros_like(model_top),
        ]
    )
    whole = merge(mine)
    model_sum, target_sum = whole[1], whole[4]
    row_kl = (
        (whole[5] - whole[6]) / target_sum - jnp.log(target_sum) + jnp.log(model_sum)
    )
    inner = (whole[2] / model_sum - whole[6] / target_sum) / (inv_rms[:, 0] * feature_count)
    prob_model = jnp.exp(logits - whole[0][:, None]) / model_sum[:, None]
    prob_target = jnp.exp(target - whole[3][:, None]) / target_sum[:, None]
    grad_logits = (prob_model - prob_target).astype(jnp.bfloat16)
    sums, moved = [], []
    for step, kz in enumerate((2, 1, 3, 0)):
        if step >= 2:
            grad_logits, sums[step - 2] = lax.optimization_barrier((grad_logits, sums[step - 2]))
            moved.append(shift(sums[step - 2], "zh", (2, 1)[step - 2]))
        blocks = list(backward(kz, grad_logits, pieces, col_count))
        if step == 1:
            blocks[3], slices = lax.optimization_barrier((blocks[3], slices))
            near = lax.dynamic_slice_in_dim(slices, zl * col_count, col_count, 2)
            far = lax.dynamic_slice_in_dim(slices, (1 - zl) * col_count, col_count, 2)
            far = shift(far, "zl", 1)
        total = blocks[0]
        for kx in (2, 1, 3):
            total = total + shift(blocks[kx], "x", kx)
        sums.append(total)
    moved.append(shift(sums[2], "zh", 3))
    slices = jnp.stack([near, far]).reshape(2, 4, 2, row_count, col_count)
    slices_own = lax.dynamic_index_in_dim(slices, c, 2, False).reshape(8 * row_count, col_count)
    slices_other = lax.dynamic_index_in_dim(slices, 1 - c, 2, False).reshape(8 * row_count, col_count)
    sums[3], moved[1], slices_own, slices_other = lax.optimization_barrier(
        (sums[3], moved[1], slices_own, slices_other)
    )
    grad_cols = sums[3] + moved[0] + moved[1] + moved[2]
    gain_cols = lax.dynamic_slice_in_dim(final_gain, first_col, col_count, 0)
    value_cols = own_part.astype(jnp.float32)
    scaled = grad_cols * gain_cols
    grad_translated = (inv_rms * scaled - value_cols * inv_rms**3 * inner[:, None]).astype(
        jnp.bfloat16
    )
    chip, other = gather_rows(grad_translated)
    over_rows = (((0,), (0,)), ((), ()))
    grad_translator = lax.dot_general(
        slices_own, chip, over_rows, preferred_element_type=jnp.float32
    )
    grad_translator, other = lax.optimization_barrier((grad_translator, other))
    grad_translator += lax.dot_general(
        slices_other, other, over_rows, preferred_element_type=jnp.float32
    )
    return (grad_translator, row_kl)


def solution(mesh):
    split = Mesh(mesh.devices.reshape(tuple(SIZES.values())), tuple(SIZES))
    return jax.shard_map(
        local,
        mesh=split,
        in_specs=(P(DP, None), P(None, VOCAB), P(), P(DP, VOCAB), P(DP, VOCAB)),
        out_specs=(P(DP, VOCAB), P(DP)),
        check_vma=False,
    )
```

```python
import functools

import jax
import jax.numpy as jnp
from jax import lax
from jax.experimental import pallas as pl
from jax.experimental.pallas import tpu as pltpu
from jax.sharding import Mesh, PartitionSpec as P

EPSILON = 1e-05
SIZES = {"zl": 2, "y": 4, "c": 2, "zh": 4, "x": 4}
DP = ("zl", "y", "c")
VOCAB = ("zh", "x")


def shift(value, axis, step):
    size = SIZES[axis]
    return lax.ppermute(value, axis, [(i, (i + step) % size) for i in range(size)])


def gather(part, unembed, hidden):
    half = unembed.shape[0] // 2
    low, high = shift(unembed, "y", 1), shift(unembed, "y", 3)
    partner = shift(unembed, "zl", 1)
    near = lax.all_gather(part, VOCAB, axis=1, tiled=True)
    low, high, partner, hidden = lax.optimization_barrier((low, high, partner, hidden))
    far_top, far_end = shift(low[:half], "y", 1), shift(high[half:], "y", 3)
    partner_low, partner_high = shift(partner, "y", 1), shift(partner, "y", 3)
    last_top, last_end = shift(partner_low[:half], "y", 1), shift(partner_high[half:], "y", 3)
    last_top, last_end, hidden = lax.optimization_barrier((last_top, last_end, hidden))
    slices = lax.all_to_all(hidden, ("y", "c"), split_axis=0, concat_axis=0, tiled=True)
    pieces = []
    for value, *spot in (
        (unembed, 0, 0, 0),
        (low, 0, 1, 0),
        (high, 0, 3, 0),
        (far_top, 0, 2, 0),
        (far_end, 0, 2, half),
        (partner, 1, 0, 0),
        (partner_low, 1, 1, 0),
        (partner_high, 1, 3, 0),
        (last_top, 1, 2, 0),
        (last_end, 1, 2, half),
    ):
        dz, dy, row = spot
        pieces += [(value, (dz, dy, 0, row)), (shift(value, "c", 1), (dz, dy, 1, row))]
    return near, pieces, slices


def position():
    return jnp.stack([lax.axis_index(a) for a in SIZES]).astype(jnp.int32)


def normalize_kernel(gain, near, normed, inverse):
    step = normed.shape[1] // 16
    total = jnp.zeros((normed.shape[0], 1), jnp.float32)
    for k in range(16):
        wide = near[:, pl.ds(k * step, step)].astype(jnp.float32)
        total += jnp.sum(wide * wide, axis=1, keepdims=True)
    inv_rms = lax.rsqrt(total / normed.shape[1] + EPSILON)
    inverse[...] = jnp.broadcast_to(inv_rms, inverse.shape)
    for k in range(16):
        at = pl.ds(k * step, step)
        wide = near[:, at].astype(jnp.float32)
        normed[:, at] = (wide * inv_rms * gain[:, at]).astype(normed.dtype)


def normalize(near, gain):
    rows, features = near.shape
    return pl.pallas_call(
        normalize_kernel,
        out_shape=[
            jax.ShapeDtypeStruct((rows, features), near.dtype),
            jax.ShapeDtypeStruct((rows, 128), jnp.float32),
        ],
        in_specs=[pl.BlockSpec(memory_space=pltpu.VMEM)] * 2,
        out_specs=[pl.BlockSpec(memory_space=pltpu.VMEM)] * 2,
        compiler_params=pltpu.CompilerParams(vmem_limit_bytes=24 * 2**20),
        cost_estimate=pl.CostEstimate(
            flops=6 * rows * features, bytes_accessed=4 * rows * features, transcendentals=rows
        ),
        name="normalize",
    )(gain[None], near)


def piece_block(place, spot):
    dz, dy, dc, _ = spot
    zl = (place[0] + (2 - dz)) % 2
    y = (place[1] + (4 - dy)) % 4
    c = (place[2] + (2 - dc)) % 2
    return zl * 8 + y * 2 + c


def forward_kernel(heights, spots, block, place, normed, *refs):
    count = len(heights)
    pieces, out, held, sems = refs[:count], refs[count], refs[count + 1], refs[count + 2]
    copies, start = [], 0
    for p, height in enumerate(heights):
        copies.append(
            pltpu.make_async_copy(pieces[p], held.at[pl.ds(start, height)], sems.at[p])
        )
        copies[-1].start()
        start += height
    start = 0
    for p, height in enumerate(heights):
        copies[p].wait()
        first = piece_block(place, spots[p]) * block + spots[p][3]
        cols = normed[:, pl.ds(pl.multiple_of(first, 256), height)]
        term = jnp.dot(cols, held[pl.ds(start, height), :], preferred_element_type=jnp.float32)
        if p:
            out[...] += term
        else:
            out[...] = term
        start += height


def forward(normed, pieces, block):
    heights = [p[0].shape[0] for p in pieces]
    rows, cols = normed.shape[0], pieces[0][0].shape[1]
    spots = [p[1] for p in pieces]
    return pl.pallas_call(
        functools.partial(forward_kernel, heights, spots, block),
        out_shape=jax.ShapeDtypeStruct((rows, cols), jnp.float32),
        in_specs=[
            pl.BlockSpec(memory_space=pltpu.SMEM),
            pl.BlockSpec(memory_space=pltpu.VMEM),
        ]
        + [pl.BlockSpec(memory_space=pltpu.HBM)] * len(pieces),
        out_specs=pl.BlockSpec(memory_space=pltpu.VMEM),
        scratch_shapes=[
            pltpu.VMEM((sum(heights), cols), jnp.bfloat16),
            pltpu.SemaphoreType.DMA((len(pieces),)),
        ],
        compiler_params=pltpu.CompilerParams(vmem_limit_bytes=54 * 2**20),
        cost_estimate=pl.CostEstimate(
            flops=2 * rows * cols * sum(heights), bytes_accessed=2 * cols * sum(heights), transcendentals=0
        ),
        name="forward",
    )(position(), normed, *[p[0] for p in pieces])


def backward_kernel(kz, spots, place, grad, *refs):
    count = len(spots)
    pieces, outs, held, sems = refs[:count], refs[count : count + 4], refs[count + 4], refs[count + 5]
    order = (2, 1, 3, 0)
    for kx in order:
        wanted = ((place[3] + kz) % 4) * 4 + (place[4] + kx) % 4
        for piece, spot in zip(pieces, spots):

            @pl.when(piece_block(place, spot) == wanted)
            def _():
                pltpu.make_async_copy(
                    piece, held.at[kx, pl.ds(spot[3], piece.shape[0])], sems.at[kx]
                ).start()

    for kx in order:
        pltpu.make_async_copy(pieces[0], held.at[kx], sems.at[kx]).wait()
        outs[kx][...] = lax.dot_general(
            grad[...], held[kx], (((1,), (1,)), ((), ())), preferred_element_type=jnp.float32
        )


def backward(kz, grad, pieces, block):
    rows, cols = grad.shape
    return pl.pallas_call(
        functools.partial(backward_kernel, kz, [p[1] for p in pieces]),
        out_shape=[jax.ShapeDtypeStruct((rows, block), jnp.float32)] * 4,
        in_specs=[
            pl.BlockSpec(memory_space=pltpu.SMEM),
            pl.BlockSpec(memory_space=pltpu.VMEM),
        ]
        + [pl.BlockSpec(memory_space=pltpu.HBM)] * len(pieces),
        out_specs=[pl.BlockSpec(memory_space=pltpu.VMEM)] * 4,
        scratch_shapes=[
            pltpu.VMEM((4, block, cols), jnp.bfloat16),
            pltpu.SemaphoreType.DMA((4,)),
        ],
        compiler_params=pltpu.CompilerParams(vmem_limit_bytes=50 * 2**20),
        cost_estimate=pl.CostEstimate(
            flops=8 * rows * cols * block,
            bytes_accessed=8 * cols * block + 16 * rows * block,
            transcendentals=0,
        ),
        name="backward",
    )(position(), grad, *[p[0] for p in pieces])


def merge_kernel(a, b, c, d, out):
    groups = (a, b, c, d)
    top = jnp.maximum(jnp.maximum(a[0:1], b[0:1]), jnp.maximum(c[0:1], d[0:1]))
    ttop = jnp.maximum(jnp.maximum(a[3:4], b[3:4]), jnp.maximum(c[3:4], d[3:4]))
    sums = [jnp.zeros_like(top) for _ in range(5)]
    for v in groups:
        dm, dt = v[0:1] - top, v[3:4] - ttop
        em, et = jnp.exp(dm), jnp.exp(dt)
        sums[0] += em * v[1:2]
        sums[1] += em * (v[2:3] + dm * v[1:2])
        sums[2] += et * v[4:5]
        sums[3] += et * (v[5:6] + dt * v[4:5])
        sums[4] += et * (v[6:7] + dm * v[4:5])
    for row, value in enumerate((top, sums[0], sums[1], ttop, sums[2], sums[3], sums[4], top)):
        out[row : row + 1] = value


def merge(s):
    for axis in VOCAB:
        far, low, high = shift(s, axis, 2), shift(s, axis, 1), shift(s, axis, 3)
        s = pl.pallas_call(
            merge_kernel,
            out_shape=jax.ShapeDtypeStruct(s.shape, s.dtype),
            in_specs=[pl.BlockSpec(memory_space=pltpu.VMEM)] * 4,
            out_specs=pl.BlockSpec(memory_space=pltpu.VMEM),
            compiler_params=pltpu.CompilerParams(vmem_limit_bytes=2**20),
            name="merge",
        )(s, low, high, far)
    return s


def gather_rows(part):
    rows, cols = part.shape
    y = lax.axis_index("y")
    chip = jnp.zeros((2, 4, rows, cols), part.dtype)
    for dz, dy in ((1, 2), (0, 2), (1, 1), (1, 3), (0, 1), (0, 3), (1, 0), (0, 0)):
        piece = part
        if dz or dy:
            moves = [
                (z * 4 + j, ((z + dz) % 2) * 4 + (j + dy) % 4) for z in range(2) for j in range(4)
            ]
            piece = lax.ppermute(part, ("zl", "y"), moves)
        chip = lax.dynamic_update_slice(chip, piece[None, None], (dz, (y - dy) % 4, 0, 0))
    chip = chip.reshape(8 * rows, cols)
    return chip, shift(chip, "c", 1)


def local(hidden_rows, translator, final_gain, unembed, target_logits):
    row_count, feature_count = hidden_rows.shape
    col_count = translator.shape[1]
    first_col = lax.axis_index(VOCAB) * col_count
    zl, c = lax.axis_index("zl"), lax.axis_index("c")
    own_inputs = lax.dynamic_slice_in_dim(hidden_rows, first_col, col_count, 1).astype(jnp.float32)
    own_part = (
        own_inputs + jnp.dot(hidden_rows, translator, preferred_element_type=jnp.float32)
    ).astype(jnp.bfloat16)
    hidden_blocks = hidden_rows.reshape(row_count, 2, 8, col_count).transpose(2, 1, 0, 3)
    hidden_blocks = hidden_blocks.reshape(8, 2 * row_count, col_count)
    near, pieces, slices = gather(own_part, unembed, hidden_blocks)
    normed, inverse = normalize(near, final_gain)
    inv_rms = inverse[:, :1]
    target = target_logits.astype(jnp.float32)
    target_top = jnp.max(target, axis=1)
    target_off = target - target_top[:, None]
    target_exp = jnp.exp(target_off)
    target_total = jnp.sum(target_exp, axis=1)
    target_mean = jnp.sum(target_exp * target_off, axis=1)
    logits = forward(normed, pieces, unembed.shape[0])
    model_top = jnp.max(logits, axis=1)
    model_off = logits - model_top[:, None]
    model_exp = jnp.exp(model_off)
    mine = jnp.stack(
        [
            model_top,
            jnp.sum(model_exp, axis=1),
            jnp.sum(model_exp * model_off, axis=1),
            target_top,
            target_total,
            target_mean,
            jnp.sum(target_exp * model_off, axis=1),
            jnp.zeros_like(model_top),
        ]
    )
    whole = merge(mine)
    model_sum, target_sum = whole[1], whole[4]
    row_kl = (
        (whole[5] - whole[6]) / target_sum - jnp.log(target_sum) + jnp.log(model_sum)
    )
    inner = (whole[2] / model_sum - whole[6] / target_sum) / (inv_rms[:, 0] * feature_count)
    prob_model = jnp.exp(logits - whole[0][:, None]) / model_sum[:, None]
    prob_target = jnp.exp(target - whole[3][:, None]) / target_sum[:, None]
    grad_logits = (prob_model - prob_target).astype(jnp.bfloat16)
    sums, moved = [], []
    for step, kz in enumerate((2, 1, 3, 0)):
        if step >= 2:
            grad_logits, sums[step - 2] = lax.optimization_barrier((grad_logits, sums[step - 2]))
            moved.append(shift(sums[step - 2], "zh", (2, 1)[step - 2]))
        blocks = list(backward(kz, grad_logits, pieces, col_count))
        if step == 1:
            blocks[3], slices = lax.optimization_barrier((blocks[3], slices))
            near = lax.dynamic_slice_in_dim(slices, zl * row_count, row_count, 1)
            far = lax.dynamic_slice_in_dim(slices, (1 - zl) * row_count, row_count, 1)
            far = shift(far, "zl", 1)
        total = blocks[0]
        for kx in (2, 1, 3):
            total = total + shift(blocks[kx], "x", kx)
        sums.append(total)
    moved.append(shift(sums[2], "zh", 3))
    slices = jnp.stack([near, far]).reshape(2, 4, 2, row_count, col_count)
    slices_own = lax.dynamic_index_in_dim(slices, c, 2, False).reshape(8 * row_count, col_count)
    slices_other = lax.dynamic_index_in_dim(slices, 1 - c, 2, False).reshape(8 * row_count, col_count)
    sums[3], moved[1], slices_own, slices_other = lax.optimization_barrier(
        (sums[3], moved[1], slices_own, slices_other)
    )
    grad_cols = sums[3] + moved[0] + moved[1] + moved[2]
    gain_cols = lax.dynamic_slice_in_dim(final_gain, first_col, col_count, 0)
    value_cols = own_part.astype(jnp.float32)
    scaled = grad_cols * gain_cols
    grad_translated = (inv_rms * scaled - value_cols * inv_rms**3 * inner[:, None]).astype(
        jnp.bfloat16
    )
    chip, other = gather_rows(grad_translated)
    over_rows = (((0,), (0,)), ((), ()))
    grad_translator = lax.dot_general(
        slices_own, chip, over_rows, preferred_element_type=jnp.float32
    )
    grad_translator, other = lax.optimization_barrier((grad_translator, other))
    grad_translator += lax.dot_general(
        slices_other, other, over_rows, preferred_element_type=jnp.float32
    )
    return (grad_translator, row_kl)


def solution(mesh):
    split = Mesh(mesh.devices.reshape(tuple(SIZES.values())), tuple(SIZES))
    return jax.shard_map(
        local,
        mesh=split,
        in_specs=(P(DP, None), P(None, VOCAB), P(), P(DP, VOCAB), P(DP, VOCAB)),
        out_specs=(P(DP, VOCAB), P(DP)),
        check_vma=False,
    )
```

```python
import functools

import jax
import jax.numpy as jnp
from jax import lax
from jax.experimental import pallas as pl
from jax.experimental.pallas import tpu as pltpu
from jax.sharding import Mesh, PartitionSpec as P

EPSILON = 1e-05
SIZES = {"zl": 2, "y": 4, "c": 2, "zh": 4, "x": 4}
DP = ("zl", "y", "c")
VOCAB = ("zh", "x")


def shift(value, axis, step):
    size = SIZES[axis]
    return lax.ppermute(value, axis, [(i, (i + step) % size) for i in range(size)])


def gather(part, unembed, hidden):
    half = unembed.shape[0] // 2
    low, high = shift(unembed, "y", 1), shift(unembed, "y", 3)
    partner = shift(unembed, "zl", 1)
    near = lax.all_gather(part, VOCAB, axis=1, tiled=True)
    low, high, partner, hidden = lax.optimization_barrier((low, high, partner, hidden))
    far_top, far_end = shift(low[:half], "y", 1), shift(high[half:], "y", 3)
    partner_low, partner_high = shift(partner, "y", 1), shift(partner, "y", 3)
    last_top, last_end = shift(partner_low[:half], "y", 1), shift(partner_high[half:], "y", 3)
    last_top, last_end, hidden = lax.optimization_barrier((last_top, last_end, hidden))
    slices = lax.all_to_all(hidden, ("y", "c"), split_axis=0, concat_axis=0, tiled=True)
    pieces = []
    for value, *spot in (
        (unembed, 0, 0, 0),
        (low, 0, 1, 0),
        (high, 0, 3, 0),
        (far_top, 0, 2, 0),
        (far_end, 0, 2, half),
        (partner, 1, 0, 0),
        (partner_low, 1, 1, 0),
        (partner_high, 1, 3, 0),
        (last_top, 1, 2, 0),
        (last_end, 1, 2, half),
    ):
        dz, dy, row = spot
        pieces += [(value, (dz, dy, 0, row)), (shift(value, "c", 1), (dz, dy, 1, row))]
    return near, pieces, slices


def position():
    return jnp.stack([lax.axis_index(a) for a in SIZES]).astype(jnp.int32)


def normalize_kernel(gain, near, normed, inverse):
    step = normed.shape[1] // 16
    total = jnp.zeros((normed.shape[0], 1), jnp.float32)
    for k in range(16):
        wide = near[:, pl.ds(k * step, step)].astype(jnp.float32)
        total += jnp.sum(wide * wide, axis=1, keepdims=True)
    inv_rms = lax.rsqrt(total / normed.shape[1] + EPSILON)
    inverse[...] = jnp.broadcast_to(inv_rms, inverse.shape)
    for k in range(16):
        at = pl.ds(k * step, step)
        wide = near[:, at].astype(jnp.float32)
        normed[:, at] = (wide * inv_rms * gain[:, at]).astype(normed.dtype)


def normalize(near, gain):
    rows, features = near.shape
    return pl.pallas_call(
        normalize_kernel,
        out_shape=[
            jax.ShapeDtypeStruct((rows, features), near.dtype),
            jax.ShapeDtypeStruct((rows, 128), jnp.float32),
        ],
        in_specs=[pl.BlockSpec(memory_space=pltpu.VMEM)] * 2,
        out_specs=[pl.BlockSpec(memory_space=pltpu.VMEM)] * 2,
        compiler_params=pltpu.CompilerParams(vmem_limit_bytes=24 * 2**20),
        cost_estimate=pl.CostEstimate(
            flops=6 * rows * features, bytes_accessed=4 * rows * features, transcendentals=rows
        ),
        name="normalize",
    )(gain[None], near)


def piece_block(place, spot):
    dz, dy, dc, _ = spot
    zl = (place[0] + (2 - dz)) % 2
    y = (place[1] + (4 - dy)) % 4
    c = (place[2] + (2 - dc)) % 2
    return zl * 8 + y * 2 + c


def forward_kernel(heights, spots, block, place, normed, *refs):
    count = len(heights)
    pieces, out, held, sems = refs[:count], refs[count], refs[count + 1], refs[count + 2]
    copies, start = [], 0
    for p, height in enumerate(heights):
        copies.append(
            pltpu.make_async_copy(pieces[p], held.at[pl.ds(start, height)], sems.at[p])
        )
        copies[-1].start()
        start += height
    start = 0
    for p, height in enumerate(heights):
        copies[p].wait()
        first = piece_block(place, spots[p]) * block + spots[p][3]
        cols = normed[:, pl.ds(pl.multiple_of(first, 256), height)]
        term = jnp.dot(cols, held[pl.ds(start, height), :], preferred_element_type=jnp.float32)
        if p:
            out[...] += term
        else:
            out[...] = term
        start += height


def forward(normed, pieces, block):
    heights = [p[0].shape[0] for p in pieces]
    rows, cols = normed.shape[0], pieces[0][0].shape[1]
    spots = [p[1] for p in pieces]
    return pl.pallas_call(
        functools.partial(forward_kernel, heights, spots, block),
        out_shape=jax.ShapeDtypeStruct((rows, cols), jnp.float32),
        in_specs=[
            pl.BlockSpec(memory_space=pltpu.SMEM),
            pl.BlockSpec(memory_space=pltpu.VMEM),
        ]
        + [pl.BlockSpec(memory_space=pltpu.HBM)] * len(pieces),
        out_specs=pl.BlockSpec(memory_space=pltpu.VMEM),
        scratch_shapes=[
            pltpu.VMEM((sum(heights), cols), jnp.bfloat16),
            pltpu.SemaphoreType.DMA((len(pieces),)),
        ],
        compiler_params=pltpu.CompilerParams(vmem_limit_bytes=54 * 2**20),
        cost_estimate=pl.CostEstimate(
            flops=2 * rows * cols * sum(heights), bytes_accessed=2 * cols * sum(heights), transcendentals=0
        ),
        name="forward",
    )(position(), normed, *[p[0] for p in pieces])


def backward_kernel(kz, spots, place, grad, *refs):
    count = len(spots)
    pieces, outs, held, sems = refs[:count], refs[count : count + 4], refs[count + 4], refs[count + 5]
    order = (2, 1, 3, 0)
    for kx in order:
        wanted = ((place[3] + kz) % 4) * 4 + (place[4] + kx) % 4
        for piece, spot in zip(pieces, spots):

            @pl.when(piece_block(place, spot) == wanted)
            def _():
                pltpu.make_async_copy(
                    piece, held.at[kx, pl.ds(spot[3], piece.shape[0])], sems.at[kx]
                ).start()

    for kx in order:
        pltpu.make_async_copy(pieces[0], held.at[kx], sems.at[kx]).wait()
        outs[kx][...] = lax.dot_general(
            grad[...], held[kx], (((1,), (1,)), ((), ())), preferred_element_type=jnp.float32
        )


def backward(kz, grad, pieces, block):
    rows, cols = grad.shape
    return pl.pallas_call(
        functools.partial(backward_kernel, kz, [p[1] for p in pieces]),
        out_shape=[jax.ShapeDtypeStruct((rows, block), jnp.float32)] * 4,
        in_specs=[
            pl.BlockSpec(memory_space=pltpu.SMEM),
            pl.BlockSpec(memory_space=pltpu.VMEM),
        ]
        + [pl.BlockSpec(memory_space=pltpu.HBM)] * len(pieces),
        out_specs=[pl.BlockSpec(memory_space=pltpu.VMEM)] * 4,
        scratch_shapes=[
            pltpu.VMEM((4, block, cols), jnp.bfloat16),
            pltpu.SemaphoreType.DMA((4,)),
        ],
        compiler_params=pltpu.CompilerParams(vmem_limit_bytes=50 * 2**20),
        cost_estimate=pl.CostEstimate(
            flops=8 * rows * cols * block,
            bytes_accessed=8 * cols * block + 16 * rows * block,
            transcendentals=0,
        ),
        name="backward",
    )(position(), grad, *[p[0] for p in pieces])


def merge_kernel(a, b, c, d, out):
    groups = (a, b, c, d)
    top = jnp.maximum(jnp.maximum(a[0:1], b[0:1]), jnp.maximum(c[0:1], d[0:1]))
    ttop = jnp.maximum(jnp.maximum(a[3:4], b[3:4]), jnp.maximum(c[3:4], d[3:4]))
    sums = [jnp.zeros_like(top) for _ in range(5)]
    for v in groups:
        dm, dt = v[0:1] - top, v[3:4] - ttop
        em, et = jnp.exp(dm), jnp.exp(dt)
        sums[0] += em * v[1:2]
        sums[1] += em * (v[2:3] + dm * v[1:2])
        sums[2] += et * v[4:5]
        sums[3] += et * (v[5:6] + dt * v[4:5])
        sums[4] += et * (v[6:7] + dm * v[4:5])
    for row, value in enumerate((top, sums[0], sums[1], ttop, sums[2], sums[3], sums[4], top)):
        out[row : row + 1] = value


def merge(s, slices):
    zl, rows = lax.axis_index("zl"), slices.shape[1] // 2
    for axis in VOCAB:
        if axis != VOCAB[0]:
            s, slices = lax.optimization_barrier((s, slices))
            near_slices = lax.dynamic_slice_in_dim(slices, zl * rows, rows, 1)
            far_slices = lax.dynamic_slice_in_dim(slices, (1 - zl) * rows, rows, 1)
            far_slices = shift(far_slices, "zl", 1)
        far, low, high = shift(s, axis, 2), shift(s, axis, 1), shift(s, axis, 3)
        s = pl.pallas_call(
            merge_kernel,
            out_shape=jax.ShapeDtypeStruct(s.shape, s.dtype),
            in_specs=[pl.BlockSpec(memory_space=pltpu.VMEM)] * 4,
            out_specs=pl.BlockSpec(memory_space=pltpu.VMEM),
            compiler_params=pltpu.CompilerParams(vmem_limit_bytes=2**20),
            name="merge",
        )(s, low, high, far)
    return s, near_slices, far_slices


def gather_rows(part):
    rows, cols = part.shape
    y = lax.axis_index("y")
    chip = jnp.zeros((2, 4, rows, cols), part.dtype)
    for dz, dy in ((1, 2), (0, 2), (1, 1), (1, 3), (0, 1), (0, 3), (1, 0), (0, 0)):
        piece = part
        if dz or dy:
            moves = [
                (z * 4 + j, ((z + dz) % 2) * 4 + (j + dy) % 4) for z in range(2) for j in range(4)
            ]
            piece = lax.ppermute(part, ("zl", "y"), moves)
        chip = lax.dynamic_update_slice(chip, piece[None, None], (dz, (y - dy) % 4, 0, 0))
    chip = chip.reshape(8 * rows, cols)
    return chip, shift(chip, "c", 1)


def local(hidden_rows, translator, final_gain, unembed, target_logits):
    row_count, feature_count = hidden_rows.shape
    col_count = translator.shape[1]
    first_col = lax.axis_index(VOCAB) * col_count
    zl, c = lax.axis_index("zl"), lax.axis_index("c")
    own_inputs = lax.dynamic_slice_in_dim(hidden_rows, first_col, col_count, 1).astype(jnp.float32)
    own_part = (
        own_inputs + jnp.dot(hidden_rows, translator, preferred_element_type=jnp.float32)
    ).astype(jnp.bfloat16)
    hidden_blocks = hidden_rows.reshape(row_count, 2, 8, col_count).transpose(2, 1, 0, 3)
    hidden_blocks = hidden_blocks.reshape(8, 2 * row_count, col_count)
    near, pieces, slices = gather(own_part, unembed, hidden_blocks)
    normed, inverse = normalize(near, final_gain)
    inv_rms = inverse[:, :1]
    target = target_logits.astype(jnp.float32)
    target_top = jnp.max(target, axis=1)
    target_off = target - target_top[:, None]
    target_exp = jnp.exp(target_off)
    target_total = jnp.sum(target_exp, axis=1)
    target_mean = jnp.sum(target_exp * target_off, axis=1)
    logits = forward(normed, pieces, unembed.shape[0])
    model_top = jnp.max(logits, axis=1)
    model_off = logits - model_top[:, None]
    model_exp = jnp.exp(model_off)
    mine = jnp.stack(
        [
            model_top,
            jnp.sum(model_exp, axis=1),
            jnp.sum(model_exp * model_off, axis=1),
            target_top,
            target_total,
            target_mean,
            jnp.sum(target_exp * model_off, axis=1),
            jnp.zeros_like(model_top),
        ]
    )
    whole, near_slices, far_slices = merge(mine, slices)
    model_sum, target_sum = whole[1], whole[4]
    row_kl = (
        (whole[5] - whole[6]) / target_sum - jnp.log(target_sum) + jnp.log(model_sum)
    )
    inner = (whole[2] / model_sum - whole[6] / target_sum) / (inv_rms[:, 0] * feature_count)
    prob_model = jnp.exp(logits - whole[0][:, None]) / model_sum[:, None]
    prob_target = jnp.exp(target - whole[3][:, None]) / target_sum[:, None]
    grad_logits = (prob_model - prob_target).astype(jnp.bfloat16)
    sums, moved = [], []
    for step, kz in enumerate((2, 1, 3, 0)):
        if step == 2:
            grad_logits, sums[0], far_slices = lax.optimization_barrier(
                (grad_logits, sums[0], far_slices)
            )
            moved.append(shift(sums[0], "zh", 2))
        if step == 3:
            grad_logits, sums[1], moved[0] = lax.optimization_barrier(
                (grad_logits, sums[1], moved[0])
            )
            moved.append(shift(sums[1], "zh", 1))
        blocks = backward(kz, grad_logits, pieces, col_count)
        total = blocks[0]
        for kx in (2, 1, 3):
            total = total + shift(blocks[kx], "x", kx)
        sums.append(total)
    sums[2], moved[1] = lax.optimization_barrier((sums[2], moved[1]))
    moved.append(shift(sums[2], "zh", 3))
    slices = jnp.stack([near_slices, far_slices]).reshape(2, 4, 2, row_count, col_count)
    slices_own = lax.dynamic_index_in_dim(slices, c, 2, False).reshape(8 * row_count, col_count)
    slices_other = lax.dynamic_index_in_dim(slices, 1 - c, 2, False).reshape(8 * row_count, col_count)
    sums[3], moved[1], slices_own, slices_other = lax.optimization_barrier(
        (sums[3], moved[1], slices_own, slices_other)
    )
    grad_cols = sums[3] + moved[0] + moved[1] + moved[2]
    gain_cols = lax.dynamic_slice_in_dim(final_gain, first_col, col_count, 0)
    value_cols = own_part.astype(jnp.float32)
    scaled = grad_cols * gain_cols
    grad_translated = (inv_rms * scaled - value_cols * inv_rms**3 * inner[:, None]).astype(
        jnp.bfloat16
    )
    chip, other = gather_rows(grad_translated)
    over_rows = (((0,), (0,)), ((), ()))
    grad_translator = lax.dot_general(
        slices_own, chip, over_rows, preferred_element_type=jnp.float32
    )
    grad_translator, other = lax.optimization_barrier((grad_translator, other))
    grad_translator += lax.dot_general(
        slices_other, other, over_rows, preferred_element_type=jnp.float32
    )
    return (grad_translator, row_kl)


def solution(mesh):
    split = Mesh(mesh.devices.reshape(tuple(SIZES.values())), tuple(SIZES))
    return jax.shard_map(
        local,
        mesh=split,
        in_specs=(P(DP, None), P(None, VOCAB), P(), P(DP, VOCAB), P(DP, VOCAB)),
        out_specs=(P(DP, VOCAB), P(DP)),
        check_vma=False,
    )
```

```python
import functools

import jax
import jax.numpy as jnp
from jax import lax
from jax.experimental import pallas as pl
from jax.experimental.pallas import tpu as pltpu
from jax.sharding import Mesh, PartitionSpec as P

EPSILON = 1e-05
SIZES = {"zl": 2, "y": 4, "c": 2, "zh": 4, "x": 4}
DP = ("zl", "y", "c")
VOCAB = ("zh", "x")


def shift(value, axis, step):
    size = SIZES[axis]
    return lax.ppermute(value, axis, [(i, (i + step) % size) for i in range(size)])


def gather(part, unembed, hidden):
    half = unembed.shape[0] // 2
    low, high = shift(unembed, "y", 1), shift(unembed, "y", 3)
    partner = shift(unembed, "zl", 1)
    near = lax.all_gather(part, VOCAB, axis=1, tiled=True)
    low, high, partner, hidden = lax.optimization_barrier((low, high, partner, hidden))
    far_top, far_end = shift(low[:half], "y", 1), shift(high[half:], "y", 3)
    partner_low, partner_high = shift(partner, "y", 1), shift(partner, "y", 3)
    last_top, last_end = shift(partner_low[:half], "y", 1), shift(partner_high[half:], "y", 3)
    last_top, last_end, hidden = lax.optimization_barrier((last_top, last_end, hidden))
    slices = lax.all_to_all(hidden, ("y", "c"), split_axis=0, concat_axis=0, tiled=True)
    pieces = []
    for value, *spot in (
        (unembed, 0, 0, 0),
        (low, 0, 1, 0),
        (high, 0, 3, 0),
        (far_top, 0, 2, 0),
        (far_end, 0, 2, half),
        (partner, 1, 0, 0),
        (partner_low, 1, 1, 0),
        (partner_high, 1, 3, 0),
        (last_top, 1, 2, 0),
        (last_end, 1, 2, half),
    ):
        dz, dy, row = spot
        pieces += [(value, (dz, dy, 0, row)), (shift(value, "c", 1), (dz, dy, 1, row))]
    return near, pieces, slices


def position():
    return jnp.stack([lax.axis_index(a) for a in SIZES]).astype(jnp.int32)


def piece_block(place, spot):
    dz, dy, dc, _ = spot
    zl = (place[0] + (2 - dz)) % 2
    y = (place[1] + (4 - dy)) % 4
    c = (place[2] + (2 - dc)) % 2
    return zl * 8 + y * 2 + c


def forward_kernel(heights, spots, block, place, gain, near, *refs):
    count = len(heights)
    pieces, out, inverse = refs[:count], refs[count], refs[count + 1]
    held, rows, normed, sems, row_sem = refs[count + 2 :]
    row_copy = pltpu.make_async_copy(near, rows, row_sem)
    row_copy.start()
    copies, start = [], 0
    for p, height in enumerate(heights):
        copies.append(
            pltpu.make_async_copy(pieces[p], held.at[pl.ds(start, height)], sems.at[p])
        )
        copies[-1].start()
        start += height
    row_copy.wait()
    total = jnp.zeros((normed.shape[0], 1), jnp.float32)
    for k in range(16):
        wide = rows[:, pl.ds(k * block, block)].astype(jnp.float32)
        total += jnp.sum(wide * wide, axis=1, keepdims=True)
    inv_rms = lax.rsqrt(total / normed.shape[1] + EPSILON)
    inverse[...] = jnp.broadcast_to(inv_rms, inverse.shape)
    for k in range(16):
        at = pl.ds(k * block, block)
        wide = rows[:, at].astype(jnp.float32)
        normed[:, at] = (wide * inv_rms * gain[:, at]).astype(normed.dtype)
    start = 0
    for p, height in enumerate(heights):
        copies[p].wait()
        first = piece_block(place, spots[p]) * block + spots[p][3]
        cols = normed[:, pl.ds(pl.multiple_of(first, 256), height)]
        term = jnp.dot(cols, held[pl.ds(start, height), :], preferred_element_type=jnp.float32)
        if p:
            out[...] += term
        else:
            out[...] = term
        start += height


def forward(near, gain, pieces, block):
    heights = [p[0].shape[0] for p in pieces]
    rows, features = near.shape
    cols = pieces[0][0].shape[1]
    spots = [p[1] for p in pieces]
    return pl.pallas_call(
        functools.partial(forward_kernel, heights, spots, block),
        out_shape=[
            jax.ShapeDtypeStruct((rows, cols), jnp.float32),
            jax.ShapeDtypeStruct((rows, 128), jnp.float32),
        ],
        in_specs=[
            pl.BlockSpec(memory_space=pltpu.SMEM),
            pl.BlockSpec(memory_space=pltpu.VMEM),
        ]
        + [pl.BlockSpec(memory_space=pltpu.HBM)] * (1 + len(pieces)),
        out_specs=[pl.BlockSpec(memory_space=pltpu.VMEM)] * 2,
        scratch_shapes=[
            pltpu.VMEM((sum(heights), cols), jnp.bfloat16),
            pltpu.VMEM((rows, features), near.dtype),
            pltpu.VMEM((rows, features), near.dtype),
            pltpu.SemaphoreType.DMA((len(pieces),)),
            pltpu.SemaphoreType.DMA,
        ],
        compiler_params=pltpu.CompilerParams(vmem_limit_bytes=54 * 2**20),
        cost_estimate=pl.CostEstimate(
            flops=2 * rows * cols * features, bytes_accessed=2 * cols * features, transcendentals=0
        ),
        name="forward",
    )(position(), gain[None], near, *[p[0] for p in pieces])


def backward_kernel(kz, spots, place, grad, *refs):
    count = len(spots)
    pieces, outs, held, sems = refs[:count], refs[count : count + 4], refs[count + 4], refs[count + 5]
    order = (2, 1, 3, 0)
    for kx in order:
        wanted = ((place[3] + kz) % 4) * 4 + (place[4] + kx) % 4
        for piece, spot in zip(pieces, spots):

            @pl.when(piece_block(place, spot) == wanted)
            def _():
                pltpu.make_async_copy(
                    piece, held.at[kx, pl.ds(spot[3], piece.shape[0])], sems.at[kx]
                ).start()

    for kx in order:
        pltpu.make_async_copy(pieces[0], held.at[kx], sems.at[kx]).wait()
        outs[kx][...] = lax.dot_general(
            grad[...], held[kx], (((1,), (1,)), ((), ())), preferred_element_type=jnp.float32
        )


def backward(kz, grad, pieces, block):
    rows, cols = grad.shape
    return pl.pallas_call(
        functools.partial(backward_kernel, kz, [p[1] for p in pieces]),
        out_shape=[jax.ShapeDtypeStruct((rows, block), jnp.float32)] * 4,
        in_specs=[
            pl.BlockSpec(memory_space=pltpu.SMEM),
            pl.BlockSpec(memory_space=pltpu.VMEM),
        ]
        + [pl.BlockSpec(memory_space=pltpu.HBM)] * len(pieces),
        out_specs=[pl.BlockSpec(memory_space=pltpu.VMEM)] * 4,
        scratch_shapes=[
            pltpu.VMEM((4, block, cols), jnp.bfloat16),
            pltpu.SemaphoreType.DMA((4,)),
        ],
        compiler_params=pltpu.CompilerParams(vmem_limit_bytes=50 * 2**20),
        cost_estimate=pl.CostEstimate(
            flops=8 * rows * cols * block,
            bytes_accessed=8 * cols * block + 16 * rows * block,
            transcendentals=0,
        ),
        name="backward",
    )(position(), grad, *[p[0] for p in pieces])


def merge_kernel(a, b, c, d, out):
    groups = (a, b, c, d)
    top = jnp.maximum(jnp.maximum(a[0:1], b[0:1]), jnp.maximum(c[0:1], d[0:1]))
    ttop = jnp.maximum(jnp.maximum(a[3:4], b[3:4]), jnp.maximum(c[3:4], d[3:4]))
    sums = [jnp.zeros_like(top) for _ in range(5)]
    for v in groups:
        dm, dt = v[0:1] - top, v[3:4] - ttop
        em, et = jnp.exp(dm), jnp.exp(dt)
        sums[0] += em * v[1:2]
        sums[1] += em * (v[2:3] + dm * v[1:2])
        sums[2] += et * v[4:5]
        sums[3] += et * (v[5:6] + dt * v[4:5])
        sums[4] += et * (v[6:7] + dm * v[4:5])
    for row, value in enumerate((top, sums[0], sums[1], ttop, sums[2], sums[3], sums[4], top)):
        out[row : row + 1] = value


def merge(s, slices):
    zl, rows = lax.axis_index("zl"), slices.shape[1] // 2
    for axis in VOCAB:
        if axis != VOCAB[0]:
            s, slices = lax.optimization_barrier((s, slices))
            near_slices = lax.dynamic_slice_in_dim(slices, zl * rows, rows, 1)
            far_slices = lax.dynamic_slice_in_dim(slices, (1 - zl) * rows, rows, 1)
            far_slices = shift(far_slices, "zl", 1)
        far, low, high = shift(s, axis, 2), shift(s, axis, 1), shift(s, axis, 3)
        s = pl.pallas_call(
            merge_kernel,
            out_shape=jax.ShapeDtypeStruct(s.shape, s.dtype),
            in_specs=[pl.BlockSpec(memory_space=pltpu.VMEM)] * 4,
            out_specs=pl.BlockSpec(memory_space=pltpu.VMEM),
            compiler_params=pltpu.CompilerParams(vmem_limit_bytes=2**20),
            name="merge",
        )(s, low, high, far)
    return s, near_slices, far_slices


def gather_rows(part):
    rows, cols = part.shape
    y = lax.axis_index("y")
    chip = jnp.zeros((2, 4, rows, cols), part.dtype)
    for dz, dy in ((1, 2), (0, 2), (1, 1), (1, 3), (0, 1), (0, 3), (1, 0), (0, 0)):
        piece = part
        if dz or dy:
            moves = [
                (z * 4 + j, ((z + dz) % 2) * 4 + (j + dy) % 4) for z in range(2) for j in range(4)
            ]
            piece = lax.ppermute(part, ("zl", "y"), moves)
        chip = lax.dynamic_update_slice(chip, piece[None, None], (dz, (y - dy) % 4, 0, 0))
    chip = chip.reshape(8 * rows, cols)
    return chip, shift(chip, "c", 1)


def local(hidden_rows, translator, final_gain, unembed, target_logits):
    row_count, feature_count = hidden_rows.shape
    col_count = translator.shape[1]
    first_col = lax.axis_index(VOCAB) * col_count
    zl, c = lax.axis_index("zl"), lax.axis_index("c")
    own_inputs = lax.dynamic_slice_in_dim(hidden_rows, first_col, col_count, 1).astype(jnp.float32)
    own_part = (
        own_inputs + jnp.dot(hidden_rows, translator, preferred_element_type=jnp.float32)
    ).astype(jnp.bfloat16)
    hidden_blocks = hidden_rows.reshape(row_count, 2, 8, col_count).transpose(2, 1, 0, 3)
    hidden_blocks = hidden_blocks.reshape(8, 2 * row_count, col_count)
    near, pieces, slices = gather(own_part, unembed, hidden_blocks)
    target = target_logits.astype(jnp.float32)
    target_top = jnp.max(target, axis=1)
    target_off = target - target_top[:, None]
    target_exp = jnp.exp(target_off)
    target_total = jnp.sum(target_exp, axis=1)
    target_mean = jnp.sum(target_exp * target_off, axis=1)
    logits, inverse = forward(near, final_gain, pieces, unembed.shape[0])
    inv_rms = inverse[:, :1]
    model_top = jnp.max(logits, axis=1)
    model_off = logits - model_top[:, None]
    model_exp = jnp.exp(model_off)
    mine = jnp.stack(
        [
            model_top,
            jnp.sum(model_exp, axis=1),
            jnp.sum(model_exp * model_off, axis=1),
            target_top,
            target_total,
            target_mean,
            jnp.sum(target_exp * model_off, axis=1),
            jnp.zeros_like(model_top),
        ]
    )
    whole, near_slices, far_slices = merge(mine, slices)
    model_sum, target_sum = whole[1], whole[4]
    row_kl = (
        (whole[5] - whole[6]) / target_sum - jnp.log(target_sum) + jnp.log(model_sum)
    )
    inner = (whole[2] / model_sum - whole[6] / target_sum) / (inv_rms[:, 0] * feature_count)
    prob_model = jnp.exp(logits - whole[0][:, None]) / model_sum[:, None]
    prob_target = jnp.exp(target - whole[3][:, None]) / target_sum[:, None]
    grad_logits = (prob_model - prob_target).astype(jnp.bfloat16)
    sums, moved = [], []
    for step, kz in enumerate((2, 1, 3, 0)):
        if step == 2:
            grad_logits, sums[0], far_slices = lax.optimization_barrier(
                (grad_logits, sums[0], far_slices)
            )
            moved.append(shift(sums[0], "zh", 2))
        if step == 3:
            grad_logits, sums[1], moved[0] = lax.optimization_barrier(
                (grad_logits, sums[1], moved[0])
            )
            moved.append(shift(sums[1], "zh", 1))
        blocks = backward(kz, grad_logits, pieces, col_count)
        total = blocks[0]
        for kx in (2, 1, 3):
            total = total + shift(blocks[kx], "x", kx)
        sums.append(total)
    sums[2], moved[1] = lax.optimization_barrier((sums[2], moved[1]))
    moved.append(shift(sums[2], "zh", 3))
    slices = jnp.stack([near_slices, far_slices]).reshape(2, 4, 2, row_count, col_count)
    slices_own = lax.dynamic_index_in_dim(slices, c, 2, False).reshape(8 * row_count, col_count)
    slices_other = lax.dynamic_index_in_dim(slices, 1 - c, 2, False).reshape(8 * row_count, col_count)
    sums[3], moved[1], slices_own, slices_other = lax.optimization_barrier(
        (sums[3], moved[1], slices_own, slices_other)
    )
    grad_cols = sums[3] + moved[0] + moved[1] + moved[2]
    gain_cols = lax.dynamic_slice_in_dim(final_gain, first_col, col_count, 0)
    value_cols = own_part.astype(jnp.float32)
    scaled = grad_cols * gain_cols
    grad_translated = (inv_rms * scaled - value_cols * inv_rms**3 * inner[:, None]).astype(
        jnp.bfloat16
    )
    chip, other = gather_rows(grad_translated)
    over_rows = (((0,), (0,)), ((), ()))
    grad_translator = lax.dot_general(
        slices_own, chip, over_rows, preferred_element_type=jnp.float32
    )
    grad_translator, other = lax.optimization_barrier((grad_translator, other))
    grad_translator += lax.dot_general(
        slices_other, other, over_rows, preferred_element_type=jnp.float32
    )
    return (grad_translator, row_kl)


def solution(mesh):
    split = Mesh(mesh.devices.reshape(tuple(SIZES.values())), tuple(SIZES))
    return jax.shard_map(
        local,
        mesh=split,
        in_specs=(P(DP, None), P(None, VOCAB), P(), P(DP, VOCAB), P(DP, VOCAB)),
        out_specs=(P(DP, VOCAB), P(DP)),
        check_vma=False,
    )
```

```python
import functools

import jax
import jax.numpy as jnp
from jax import lax
from jax.experimental import pallas as pl
from jax.experimental.pallas import tpu as pltpu
from jax.sharding import Mesh, PartitionSpec as P

EPSILON = 1e-05
SIZES = {"zl": 2, "y": 4, "c": 2, "zh": 4, "x": 4}
DP = ("zl", "y", "c")
VOCAB = ("zh", "x")


def shift(value, axis, step):
    size = SIZES[axis]
    return lax.ppermute(value, axis, [(i, (i + step) % size) for i in range(size)])


def gather(part, unembed, hidden):
    half = unembed.shape[0] // 2
    low, high = shift(unembed, "y", 1), shift(unembed, "y", 3)
    partner = shift(unembed, "zl", 1)
    near = lax.all_gather(part, VOCAB, axis=1, tiled=True)
    low, high, partner, hidden = lax.optimization_barrier((low, high, partner, hidden))
    far_top, far_end = shift(low[:half], "y", 1), shift(high[half:], "y", 3)
    partner_low, partner_high = shift(partner, "y", 1), shift(partner, "y", 3)
    early = [shift(value, "c", 1) for value in (unembed, low, high, partner)]
    partner_low, partner_high, *early = lax.optimization_barrier((partner_low, partner_high, *early))
    early = dict(zip(((0, 0), (0, 1), (0, 3), (1, 0)), early))
    last_top, last_end = shift(partner_low[:half], "y", 1), shift(partner_high[half:], "y", 3)
    last_top, last_end, far_top, far_end, hidden = lax.optimization_barrier(
        (last_top, last_end, far_top, far_end, hidden)
    )
    slices = lax.all_to_all(hidden, ("y", "c"), split_axis=0, concat_axis=0, tiled=True)
    pieces = []
    for value, *spot in (
        (unembed, 0, 0, 0),
        (low, 0, 1, 0),
        (high, 0, 3, 0),
        (far_top, 0, 2, 0),
        (far_end, 0, 2, half),
        (partner, 1, 0, 0),
        (partner_low, 1, 1, 0),
        (partner_high, 1, 3, 0),
        (last_top, 1, 2, 0),
        (last_end, 1, 2, half),
    ):
        dz, dy, row = spot
        other = early[dz, dy] if (dz, dy) in early else shift(value, "c", 1)
        pieces += [(value, (dz, dy, 0, row)), (other, (dz, dy, 1, row))]
    return near, pieces, slices


def position():
    return jnp.stack([lax.axis_index(a) for a in SIZES]).astype(jnp.int32)


def normalize_kernel(gain, near, normed, inverse):
    step = normed.shape[1] // 16
    total = jnp.zeros((normed.shape[0], 1), jnp.float32)
    for k in range(16):
        wide = near[:, pl.ds(k * step, step)].astype(jnp.float32)
        total += jnp.sum(wide * wide, axis=1, keepdims=True)
    inv_rms = lax.rsqrt(total / normed.shape[1] + EPSILON)
    inverse[...] = jnp.broadcast_to(inv_rms, inverse.shape)
    for k in range(16):
        at = pl.ds(k * step, step)
        wide = near[:, at].astype(jnp.float32)
        normed[:, at] = (wide * inv_rms * gain[:, at]).astype(normed.dtype)


def normalize(near, gain):
    rows, features = near.shape
    return pl.pallas_call(
        normalize_kernel,
        out_shape=[
            jax.ShapeDtypeStruct((rows, features), near.dtype),
            jax.ShapeDtypeStruct((rows, 128), jnp.float32),
        ],
        in_specs=[pl.BlockSpec(memory_space=pltpu.VMEM)] * 2,
        out_specs=[pl.BlockSpec(memory_space=pltpu.VMEM)] * 2,
        compiler_params=pltpu.CompilerParams(vmem_limit_bytes=24 * 2**20),
        cost_estimate=pl.CostEstimate(
            flops=6 * rows * features, bytes_accessed=4 * rows * features, transcendentals=rows
        ),
        name="normalize",
    )(gain[None], near)


def piece_block(place, spot):
    dz, dy, dc, _ = spot
    zl = (place[0] + (2 - dz)) % 2
    y = (place[1] + (4 - dy)) % 4
    c = (place[2] + (2 - dc)) % 2
    return zl * 8 + y * 2 + c


def forward_kernel(heights, spots, block, place, normed, *refs):
    count = len(heights)
    pieces, out, held, sems = refs[:count], refs[count], refs[count + 1], refs[count + 2]
    copies, start = [], 0
    for p, height in enumerate(heights):
        copies.append(
            pltpu.make_async_copy(pieces[p], held.at[pl.ds(start, height)], sems.at[p])
        )
        copies[-1].start()
        start += height
    start = 0
    for p, height in enumerate(heights):
        copies[p].wait()
        first = piece_block(place, spots[p]) * block + spots[p][3]
        cols = normed[:, pl.ds(pl.multiple_of(first, 256), height)]
        term = jnp.dot(cols, held[pl.ds(start, height), :], preferred_element_type=jnp.float32)
        if p:
            out[...] += term
        else:
            out[...] = term
        start += height


def forward(normed, pieces, block):
    heights = [p[0].shape[0] for p in pieces]
    rows, cols = normed.shape[0], pieces[0][0].shape[1]
    spots = [p[1] for p in pieces]
    return pl.pallas_call(
        functools.partial(forward_kernel, heights, spots, block),
        out_shape=jax.ShapeDtypeStruct((rows, cols), jnp.float32),
        in_specs=[
            pl.BlockSpec(memory_space=pltpu.SMEM),
            pl.BlockSpec(memory_space=pltpu.VMEM),
        ]
        + [pl.BlockSpec(memory_space=pltpu.HBM)] * len(pieces),
        out_specs=pl.BlockSpec(memory_space=pltpu.VMEM),
        scratch_shapes=[
            pltpu.VMEM((sum(heights), cols), jnp.bfloat16),
            pltpu.SemaphoreType.DMA((len(pieces),)),
        ],
        compiler_params=pltpu.CompilerParams(vmem_limit_bytes=54 * 2**20),
        cost_estimate=pl.CostEstimate(
            flops=2 * rows * cols * sum(heights), bytes_accessed=2 * cols * sum(heights), transcendentals=0
        ),
        name="forward",
    )(position(), normed, *[p[0] for p in pieces])


def backward_kernel(kz, spots, place, grad, *refs):
    count = len(spots)
    pieces, outs, held, sems = refs[:count], refs[count : count + 4], refs[count + 4], refs[count + 5]
    order = (2, 1, 3, 0)
    for kx in order:
        wanted = ((place[3] + kz) % 4) * 4 + (place[4] + kx) % 4
        for piece, spot in zip(pieces, spots):

            @pl.when(piece_block(place, spot) == wanted)
            def _():
                pltpu.make_async_copy(
                    piece, held.at[kx, pl.ds(spot[3], piece.shape[0])], sems.at[kx]
                ).start()

    for kx in order:
        pltpu.make_async_copy(pieces[0], held.at[kx], sems.at[kx]).wait()
        outs[kx][...] = lax.dot_general(
            grad[...], held[kx], (((1,), (1,)), ((), ())), preferred_element_type=jnp.float32
        )


def backward(kz, grad, pieces, block):
    rows, cols = grad.shape
    return pl.pallas_call(
        functools.partial(backward_kernel, kz, [p[1] for p in pieces]),
        out_shape=[jax.ShapeDtypeStruct((rows, block), jnp.float32)] * 4,
        in_specs=[
            pl.BlockSpec(memory_space=pltpu.SMEM),
            pl.BlockSpec(memory_space=pltpu.VMEM),
        ]
        + [pl.BlockSpec(memory_space=pltpu.HBM)] * len(pieces),
        out_specs=[pl.BlockSpec(memory_space=pltpu.VMEM)] * 4,
        scratch_shapes=[
            pltpu.VMEM((4, block, cols), jnp.bfloat16),
            pltpu.SemaphoreType.DMA((4,)),
        ],
        compiler_params=pltpu.CompilerParams(vmem_limit_bytes=50 * 2**20),
        cost_estimate=pl.CostEstimate(
            flops=8 * rows * cols * block,
            bytes_accessed=8 * cols * block + 16 * rows * block,
            transcendentals=0,
        ),
        name="backward",
    )(position(), grad, *[p[0] for p in pieces])


def merge_kernel(a, b, c, d, out):
    groups = (a, b, c, d)
    top = jnp.maximum(jnp.maximum(a[0:1], b[0:1]), jnp.maximum(c[0:1], d[0:1]))
    ttop = jnp.maximum(jnp.maximum(a[3:4], b[3:4]), jnp.maximum(c[3:4], d[3:4]))
    sums = [jnp.zeros_like(top) for _ in range(5)]
    for v in groups:
        dm, dt = v[0:1] - top, v[3:4] - ttop
        em, et = jnp.exp(dm), jnp.exp(dt)
        sums[0] += em * v[1:2]
        sums[1] += em * (v[2:3] + dm * v[1:2])
        sums[2] += et * v[4:5]
        sums[3] += et * (v[5:6] + dt * v[4:5])
        sums[4] += et * (v[6:7] + dm * v[4:5])
    for row, value in enumerate((top, sums[0], sums[1], ttop, sums[2], sums[3], sums[4], top)):
        out[row : row + 1] = value


def merge(s, slices):
    zl, rows = lax.axis_index("zl"), slices.shape[1] // 2
    for axis in VOCAB:
        if axis != VOCAB[0]:
            s, slices = lax.optimization_barrier((s, slices))
            near_slices = lax.dynamic_slice_in_dim(slices, zl * rows, rows, 1)
            far_slices = lax.dynamic_slice_in_dim(slices, (1 - zl) * rows, rows, 1)
            far_slices = shift(far_slices, "zl", 1)
        far, low, high = shift(s, axis, 2), shift(s, axis, 1), shift(s, axis, 3)
        s = pl.pallas_call(
            merge_kernel,
            out_shape=jax.ShapeDtypeStruct(s.shape, s.dtype),
            in_specs=[pl.BlockSpec(memory_space=pltpu.VMEM)] * 4,
            out_specs=pl.BlockSpec(memory_space=pltpu.VMEM),
            compiler_params=pltpu.CompilerParams(vmem_limit_bytes=2**20),
            name="merge",
        )(s, low, high, far)
    return s, near_slices, far_slices


def gather_rows(part):
    rows, cols = part.shape
    y = lax.axis_index("y")
    chip = jnp.zeros((2, 4, rows, cols), part.dtype)
    for dz, dy in ((1, 2), (0, 2), (1, 1), (1, 3), (0, 1), (0, 3), (1, 0), (0, 0)):
        piece = part
        if dz or dy:
            moves = [
                (z * 4 + j, ((z + dz) % 2) * 4 + (j + dy) % 4) for z in range(2) for j in range(4)
            ]
            piece = lax.ppermute(part, ("zl", "y"), moves)
        chip = lax.dynamic_update_slice(chip, piece[None, None], (dz, (y - dy) % 4, 0, 0))
    chip = chip.reshape(8 * rows, cols)
    return chip, shift(chip, "c", 1)


def local(hidden_rows, translator, final_gain, unembed, target_logits):
    row_count, feature_count = hidden_rows.shape
    col_count = translator.shape[1]
    first_col = lax.axis_index(VOCAB) * col_count
    zl, c = lax.axis_index("zl"), lax.axis_index("c")
    own_inputs = lax.dynamic_slice_in_dim(hidden_rows, first_col, col_count, 1).astype(jnp.float32)
    own_part = (
        own_inputs + jnp.dot(hidden_rows, translator, preferred_element_type=jnp.float32)
    ).astype(jnp.bfloat16)
    hidden_blocks = hidden_rows.reshape(row_count, 2, 8, col_count).transpose(2, 1, 0, 3)
    hidden_blocks = hidden_blocks.reshape(8, 2 * row_count, col_count)
    near, pieces, slices = gather(own_part, unembed, hidden_blocks)
    normed, inverse = normalize(near, final_gain)
    inv_rms = inverse[:, :1]
    target = target_logits.astype(jnp.float32)
    target_top = jnp.max(target, axis=1)
    target_off = target - target_top[:, None]
    target_exp = jnp.exp(target_off)
    target_total = jnp.sum(target_exp, axis=1)
    target_mean = jnp.sum(target_exp * target_off, axis=1)
    logits = forward(normed, pieces, unembed.shape[0])
    model_top = jnp.max(logits, axis=1)
    model_off = logits - model_top[:, None]
    model_exp = jnp.exp(model_off)
    mine = jnp.stack(
        [
            model_top,
            jnp.sum(model_exp, axis=1),
            jnp.sum(model_exp * model_off, axis=1),
            target_top,
            target_total,
            target_mean,
            jnp.sum(target_exp * model_off, axis=1),
            jnp.zeros_like(model_top),
        ]
    )
    whole, near_slices, far_slices = merge(mine, slices)
    model_sum, target_sum = whole[1], whole[4]
    row_kl = (
        (whole[5] - whole[6]) / target_sum - jnp.log(target_sum) + jnp.log(model_sum)
    )
    inner = (whole[2] / model_sum - whole[6] / target_sum) / (inv_rms[:, 0] * feature_count)
    prob_model = jnp.exp(logits - whole[0][:, None]) / model_sum[:, None]
    prob_target = jnp.exp(target - whole[3][:, None]) / target_sum[:, None]
    grad_logits = (prob_model - prob_target).astype(jnp.bfloat16)
    sums, moved = [], []
    for step, kz in enumerate((2, 1, 3, 0)):
        if step == 2:
            grad_logits, sums[0], far_slices = lax.optimization_barrier(
                (grad_logits, sums[0], far_slices)
            )
            moved.append(shift(sums[0], "zh", 2))
        if step == 3:
            grad_logits, sums[1], moved[0] = lax.optimization_barrier(
                (grad_logits, sums[1], moved[0])
            )
            moved.append(shift(sums[1], "zh", 1))
        blocks = backward(kz, grad_logits, pieces, col_count)
        total = blocks[0]
        for kx in (2, 1, 3):
            total = total + shift(blocks[kx], "x", kx)
        sums.append(total)
    sums[2], moved[1] = lax.optimization_barrier((sums[2], moved[1]))
    moved.append(shift(sums[2], "zh", 3))
    slices = jnp.stack([near_slices, far_slices]).reshape(2, 4, 2, row_count, col_count)
    slices_own = lax.dynamic_index_in_dim(slices, c, 2, False).reshape(8 * row_count, col_count)
    slices_other = lax.dynamic_index_in_dim(slices, 1 - c, 2, False).reshape(8 * row_count, col_count)
    sums[3], moved[1], slices_own, slices_other = lax.optimization_barrier(
        (sums[3], moved[1], slices_own, slices_other)
    )
    grad_cols = sums[3] + moved[0] + moved[1] + moved[2]
    gain_cols = lax.dynamic_slice_in_dim(final_gain, first_col, col_count, 0)
    value_cols = own_part.astype(jnp.float32)
    scaled = grad_cols * gain_cols
    grad_translated = (inv_rms * scaled - value_cols * inv_rms**3 * inner[:, None]).astype(
        jnp.bfloat16
    )
    chip, other = gather_rows(grad_translated)
    over_rows = (((0,), (0,)), ((), ()))
    grad_translator = lax.dot_general(
        slices_own, chip, over_rows, preferred_element_type=jnp.float32
    )
    grad_translator, other = lax.optimization_barrier((grad_translator, other))
    grad_translator += lax.dot_general(
        slices_other, other, over_rows, preferred_element_type=jnp.float32
    )
    return (grad_translator, row_kl)


def solution(mesh):
    split = Mesh(mesh.devices.reshape(tuple(SIZES.values())), tuple(SIZES))
    return jax.shard_map(
        local,
        mesh=split,
        in_specs=(P(DP, None), P(None, VOCAB), P(), P(DP, VOCAB), P(DP, VOCAB)),
        out_specs=(P(DP, VOCAB), P(DP)),
        check_vma=False,
    )
```

```python
import functools

import jax
import jax.numpy as jnp
from jax import lax
from jax.experimental import pallas as pl
from jax.experimental.pallas import tpu as pltpu
from jax.sharding import Mesh, PartitionSpec as P

EPSILON = 1e-05
SIZES = {"zl": 2, "y": 4, "c": 2, "zh": 4, "x": 4}
DP = ("zl", "y", "c")
VOCAB = ("zh", "x")


def shift(value, axis, step):
    size = SIZES[axis]
    return lax.ppermute(value, axis, [(i, (i + step) % size) for i in range(size)])


def gather(part, unembed, hidden):
    half = unembed.shape[0] // 2
    low, high = shift(unembed, "y", 1), shift(unembed, "y", 3)
    partner = shift(unembed, "zl", 1)
    near = lax.all_gather(part, VOCAB, axis=1, tiled=True)
    low, high, partner, hidden = lax.optimization_barrier((low, high, partner, hidden))
    far_top, far_end = shift(low[:half], "y", 1), shift(high[half:], "y", 3)
    partner_low, partner_high = shift(partner, "y", 1), shift(partner, "y", 3)
    early = [shift(value, "c", 1) for value in (unembed, low, high, partner)]
    partner_low, partner_high, *early = lax.optimization_barrier((partner_low, partner_high, *early))
    early = dict(zip(((0, 0), (0, 1), (0, 3), (1, 0)), early))
    last_top, last_end = shift(partner_low[:half], "y", 1), shift(partner_high[half:], "y", 3)
    last_top, last_end, far_top, far_end, hidden = lax.optimization_barrier(
        (last_top, last_end, far_top, far_end, hidden)
    )
    slices = lax.all_to_all(hidden, ("y", "c"), split_axis=0, concat_axis=0, tiled=True)
    pieces = []
    for value, *spot in (
        (unembed, 0, 0, 0),
        (low, 0, 1, 0),
        (high, 0, 3, 0),
        (far_top, 0, 2, 0),
        (far_end, 0, 2, half),
        (partner, 1, 0, 0),
        (partner_low, 1, 1, 0),
        (partner_high, 1, 3, 0),
        (last_top, 1, 2, 0),
        (last_end, 1, 2, half),
    ):
        dz, dy, row = spot
        other = early[dz, dy] if (dz, dy) in early else shift(value, "c", 1)
        pieces += [(value, (dz, dy, 0, row)), (other, (dz, dy, 1, row))]
    return near, pieces, slices


def position():
    return jnp.stack([lax.axis_index(a) for a in SIZES]).astype(jnp.int32)


def normalize_kernel(gain, near, normed, inverse):
    step = normed.shape[1] // 16
    total = jnp.zeros((normed.shape[0], 1), jnp.float32)
    for k in range(16):
        wide = near[:, pl.ds(k * step, step)].astype(jnp.float32)
        total += jnp.sum(wide * wide, axis=1, keepdims=True)
    inv_rms = lax.rsqrt(total / normed.shape[1] + EPSILON)
    inverse[...] = jnp.broadcast_to(inv_rms, inverse.shape)
    for k in range(16):
        at = pl.ds(k * step, step)
        wide = near[:, at].astype(jnp.float32)
        normed[:, at] = (wide * inv_rms * gain[:, at]).astype(normed.dtype)


def normalize(near, gain):
    rows, features = near.shape
    return pl.pallas_call(
        normalize_kernel,
        out_shape=[
            jax.ShapeDtypeStruct((rows, features), near.dtype),
            jax.ShapeDtypeStruct((rows, 128), jnp.float32),
        ],
        in_specs=[pl.BlockSpec(memory_space=pltpu.VMEM)] * 2,
        out_specs=[pl.BlockSpec(memory_space=pltpu.VMEM)] * 2,
        compiler_params=pltpu.CompilerParams(vmem_limit_bytes=24 * 2**20),
        cost_estimate=pl.CostEstimate(
            flops=6 * rows * features, bytes_accessed=4 * rows * features, transcendentals=rows
        ),
        name="normalize",
    )(gain[None], near)


def piece_block(place, spot):
    dz, dy, dc, _ = spot
    zl = (place[0] + (2 - dz)) % 2
    y = (place[1] + (4 - dy)) % 4
    c = (place[2] + (2 - dc)) % 2
    return zl * 8 + y * 2 + c


def forward_kernel(heights, spots, block, place, normed, *refs):
    count = len(heights)
    pieces, out, held, sems = refs[:count], refs[count], refs[count + 1], refs[count + 2]
    copies, start = [], 0
    for p, height in enumerate(heights):
        copies.append(
            pltpu.make_async_copy(pieces[p], held.at[pl.ds(start, height)], sems.at[p])
        )
        copies[-1].start()
        start += height
    start = 0
    for p, height in enumerate(heights):
        copies[p].wait()
        first = piece_block(place, spots[p]) * block + spots[p][3]
        cols = normed[:, pl.ds(pl.multiple_of(first, 256), height)]
        term = jnp.dot(cols, held[pl.ds(start, height), :], preferred_element_type=jnp.float32)
        if p:
            out[...] += term
        else:
            out[...] = term
        start += height


def forward(normed, pieces, block):
    heights = [p[0].shape[0] for p in pieces]
    rows, cols = normed.shape[0], pieces[0][0].shape[1]
    spots = [p[1] for p in pieces]
    return pl.pallas_call(
        functools.partial(forward_kernel, heights, spots, block),
        out_shape=jax.ShapeDtypeStruct((rows, cols), jnp.float32),
        in_specs=[
            pl.BlockSpec(memory_space=pltpu.SMEM),
            pl.BlockSpec(memory_space=pltpu.VMEM),
        ]
        + [pl.BlockSpec(memory_space=pltpu.HBM)] * len(pieces),
        out_specs=pl.BlockSpec(memory_space=pltpu.VMEM),
        scratch_shapes=[
            pltpu.VMEM((sum(heights), cols), jnp.bfloat16),
            pltpu.SemaphoreType.DMA((len(pieces),)),
        ],
        compiler_params=pltpu.CompilerParams(vmem_limit_bytes=54 * 2**20),
        cost_estimate=pl.CostEstimate(
            flops=2 * rows * cols * sum(heights), bytes_accessed=2 * cols * sum(heights), transcendentals=0
        ),
        name="forward",
    )(position(), normed, *[p[0] for p in pieces])


def backward_kernel(kz, spots, place, grad, *refs):
    count = len(spots)
    pieces, outs, held, sems = refs[:count], refs[count : count + 4], refs[count + 4], refs[count + 5]
    order = (2, 1, 3, 0)
    for kx in order:
        wanted = ((place[3] + kz) % 4) * 4 + (place[4] + kx) % 4
        for piece, spot in zip(pieces, spots):

            @pl.when(piece_block(place, spot) == wanted)
            def _():
                pltpu.make_async_copy(
                    piece, held.at[kx, pl.ds(spot[3], piece.shape[0])], sems.at[kx]
                ).start()

    for kx in order:
        pltpu.make_async_copy(pieces[0], held.at[kx], sems.at[kx]).wait()
        outs[kx][...] = lax.dot_general(
            grad[...], held[kx], (((1,), (1,)), ((), ())), preferred_element_type=jnp.float32
        )


def backward(kz, grad, pieces, block):
    rows, cols = grad.shape
    return pl.pallas_call(
        functools.partial(backward_kernel, kz, [p[1] for p in pieces]),
        out_shape=[jax.ShapeDtypeStruct((rows, block), jnp.float32)] * 4,
        in_specs=[
            pl.BlockSpec(memory_space=pltpu.SMEM),
            pl.BlockSpec(memory_space=pltpu.VMEM),
        ]
        + [pl.BlockSpec(memory_space=pltpu.HBM)] * len(pieces),
        out_specs=[pl.BlockSpec(memory_space=pltpu.VMEM)] * 4,
        scratch_shapes=[
            pltpu.VMEM((4, block, cols), jnp.bfloat16),
            pltpu.SemaphoreType.DMA((4,)),
        ],
        compiler_params=pltpu.CompilerParams(vmem_limit_bytes=50 * 2**20),
        cost_estimate=pl.CostEstimate(
            flops=8 * rows * cols * block,
            bytes_accessed=8 * cols * block + 16 * rows * block,
            transcendentals=0,
        ),
        name="backward",
    )(position(), grad, *[p[0] for p in pieces])


def merge_kernel(a, b, c, d, out):
    groups = (a, b, c, d)
    top = jnp.maximum(jnp.maximum(a[0:1], b[0:1]), jnp.maximum(c[0:1], d[0:1]))
    ttop = jnp.maximum(jnp.maximum(a[3:4], b[3:4]), jnp.maximum(c[3:4], d[3:4]))
    sums = [jnp.zeros_like(top) for _ in range(5)]
    for v in groups:
        dm, dt = v[0:1] - top, v[3:4] - ttop
        em, et = jnp.exp(dm), jnp.exp(dt)
        sums[0] += em * v[1:2]
        sums[1] += em * (v[2:3] + dm * v[1:2])
        sums[2] += et * v[4:5]
        sums[3] += et * (v[5:6] + dt * v[4:5])
        sums[4] += et * (v[6:7] + dm * v[4:5])
    for row, value in enumerate((top, sums[0], sums[1], ttop, sums[2], sums[3], sums[4], top)):
        out[row : row + 1] = value


def merge(s, slices):
    zl, rows = lax.axis_index("zl"), slices.shape[1] // 2
    for axis in VOCAB:
        if axis != VOCAB[0]:
            s, slices = lax.optimization_barrier((s, slices))
            far_slices = lax.dynamic_slice_in_dim(slices, (1 - zl) * rows, rows, 1)
            far_slices = shift(far_slices, "zl", 1)
        far, low, high = shift(s, axis, 2), shift(s, axis, 1), shift(s, axis, 3)
        s = pl.pallas_call(
            merge_kernel,
            out_shape=jax.ShapeDtypeStruct(s.shape, s.dtype),
            in_specs=[pl.BlockSpec(memory_space=pltpu.VMEM)] * 4,
            out_specs=pl.BlockSpec(memory_space=pltpu.VMEM),
            compiler_params=pltpu.CompilerParams(vmem_limit_bytes=2**20),
            name="merge",
        )(s, low, high, far)
    return s, slices, far_slices


def gather_rows(part):
    rows, cols = part.shape
    y = lax.axis_index("y")
    chip = jnp.zeros((2, 4, rows, cols), part.dtype)
    for dz, dy in ((1, 2), (0, 2), (1, 1), (1, 3), (0, 1), (0, 3), (1, 0), (0, 0)):
        piece = part
        if dz or dy:
            moves = [
                (z * 4 + j, ((z + dz) % 2) * 4 + (j + dy) % 4) for z in range(2) for j in range(4)
            ]
            piece = lax.ppermute(part, ("zl", "y"), moves)
        chip = lax.dynamic_update_slice(chip, piece[None, None], (dz, (y - dy) % 4, 0, 0))
    chip = chip.reshape(8 * rows, cols)
    return chip, shift(chip, "c", 1)


def local(hidden_rows, translator, final_gain, unembed, target_logits):
    row_count, feature_count = hidden_rows.shape
    col_count = translator.shape[1]
    first_col = lax.axis_index(VOCAB) * col_count
    zl, c = lax.axis_index("zl"), lax.axis_index("c")
    own_inputs = lax.dynamic_slice_in_dim(hidden_rows, first_col, col_count, 1).astype(jnp.float32)
    own_part = (
        own_inputs + jnp.dot(hidden_rows, translator, preferred_element_type=jnp.float32)
    ).astype(jnp.bfloat16)
    hidden_blocks = hidden_rows.reshape(row_count, 2, 8, col_count).transpose(2, 1, 0, 3)
    hidden_blocks = hidden_blocks.reshape(8, 2 * row_count, col_count)
    near, pieces, slices = gather(own_part, unembed, hidden_blocks)
    normed, inverse = normalize(near, final_gain)
    inv_rms = inverse[:, :1]
    target = target_logits.astype(jnp.float32)
    target_top = jnp.max(target, axis=1)
    target_off = target - target_top[:, None]
    target_exp = jnp.exp(target_off)
    target_total = jnp.sum(target_exp, axis=1)
    target_mean = jnp.sum(target_exp * target_off, axis=1)
    logits = forward(normed, pieces, unembed.shape[0])
    model_top = jnp.max(logits, axis=1)
    model_off = logits - model_top[:, None]
    model_exp = jnp.exp(model_off)
    mine = jnp.stack(
        [
            model_top,
            jnp.sum(model_exp, axis=1),
            jnp.sum(model_exp * model_off, axis=1),
            target_top,
            target_total,
            target_mean,
            jnp.sum(target_exp * model_off, axis=1),
            jnp.zeros_like(model_top),
        ]
    )
    whole, slices, far_slices = merge(mine, slices)
    model_sum, target_sum = whole[1], whole[4]
    row_kl = (
        (whole[5] - whole[6]) / target_sum - jnp.log(target_sum) + jnp.log(model_sum)
    )
    inner = (whole[2] / model_sum - whole[6] / target_sum) / (inv_rms[:, 0] * feature_count)
    prob_model = jnp.exp(logits - whole[0][:, None]) / model_sum[:, None]
    prob_target = jnp.exp(target - whole[3][:, None]) / target_sum[:, None]
    grad_logits = (prob_model - prob_target).astype(jnp.bfloat16)
    sums, moved = [], []
    for step, kz in enumerate((2, 1, 3, 0)):
        if step == 2:
            grad_logits, sums[0], far_slices, slices = lax.optimization_barrier(
                (grad_logits, sums[0], far_slices, slices)
            )
            near_slices = lax.dynamic_slice_in_dim(slices, zl * row_count, row_count, 1)
            moved.append(shift(sums[0], "zh", 2))
        if step == 3:
            grad_logits, sums[1], moved[0] = lax.optimization_barrier(
                (grad_logits, sums[1], moved[0])
            )
            moved.append(shift(sums[1], "zh", 1))
        blocks = backward(kz, grad_logits, pieces, col_count)
        total = blocks[0]
        for kx in (2, 1, 3):
            total = total + shift(blocks[kx], "x", kx)
        sums.append(total)
    sums[2], moved[1] = lax.optimization_barrier((sums[2], moved[1]))
    moved.append(shift(sums[2], "zh", 3))
    slices = jnp.stack([near_slices, far_slices]).reshape(2, 4, 2, row_count, col_count)
    slices_own = lax.dynamic_index_in_dim(slices, c, 2, False).reshape(8 * row_count, col_count)
    slices_other = lax.dynamic_index_in_dim(slices, 1 - c, 2, False).reshape(8 * row_count, col_count)
    sums[3], moved[1], slices_own, slices_other = lax.optimization_barrier(
        (sums[3], moved[1], slices_own, slices_other)
    )
    grad_cols = sums[3] + moved[0] + moved[1] + moved[2]
    gain_cols = lax.dynamic_slice_in_dim(final_gain, first_col, col_count, 0)
    value_cols = own_part.astype(jnp.float32)
    scaled = grad_cols * gain_cols
    grad_translated = (inv_rms * scaled - value_cols * inv_rms**3 * inner[:, None]).astype(
        jnp.bfloat16
    )
    chip, other = gather_rows(grad_translated)
    over_rows = (((0,), (0,)), ((), ()))
    grad_translator = lax.dot_general(
        slices_own, chip, over_rows, preferred_element_type=jnp.float32
    )
    grad_translator, other = lax.optimization_barrier((grad_translator, other))
    grad_translator += lax.dot_general(
        slices_other, other, over_rows, preferred_element_type=jnp.float32
    )
    return (grad_translator, row_kl)


def solution(mesh):
    split = Mesh(mesh.devices.reshape(tuple(SIZES.values())), tuple(SIZES))
    return jax.shard_map(
        local,
        mesh=split,
        in_specs=(P(DP, None), P(None, VOCAB), P(), P(DP, VOCAB), P(DP, VOCAB)),
        out_specs=(P(DP, VOCAB), P(DP)),
        check_vma=False,
    )
```
